32 devices in a mesh: pool: 2 (over y), ctx: 4 (over x, core), head: 4 (over z).
Axes of the slice: x: 2, y: 2, z: 4, core: 2. Of those that a mesh axis runs over, the one named last changes fastest.
Arguments:
- kv_pool: bfloat16 [4, 64, 2, 32, 1024], P('ctx', 'pool', None, None, 'head'), may hold values from -6 to 6
- state_pool: bfloat16 [64, 64, 1024], P('pool', 'ctx', 'head'), may hold values from -0.59765625 to 0.59765625
- block_owner: int32 [4, 64], P('ctx'), may hold values from 0 to 1, as said below
- block_index: int32 [4, 64], P('ctx'), may hold values from 0 to 31, as said below
- history_len: int32 [2], P('pool'), may hold values from 1 to 4096, as said below
- turn_len: int32 [2], P('pool'), may hold values from 256 to 512, as said below
- mixer_in: bfloat16 [2, 128, 64, 512], P('pool', 'head', 'ctx'), may hold values from -6 to 6
- input_proj: bfloat16 [2, 8, 256, 512], P('pool', 'head'), may hold values from -1.5 to 1.5
- output_proj: bfloat16 [2, 8, 256, 512], P('pool', 'head'), may hold values from -6 to 6
- step_size: float32 [2, 128, 512], P('pool', 'head'), may hold values from 0 to 2, as said below
- decay_rate: float32 [128], P('head'), may hold values from 0 to 4, as said below
- bypass_factor: float32 [128], P('head'), may hold values from 0.5 to 1.5
- queries: bfloat16 [2, 512, 8192], P('pool', 'ctx', 'head'), may hold values from -300 to 300
- turn_kv: bfloat16 [2, 2, 512, 1024], P('pool', None, 'ctx', 'head'), may hold values from -6 to 6
Outputs:
- mixer_out: bfloat16 [2, 128, 64, 512], P('pool', 'head', 'ctx')
- next_state: float32 [2, 128, 64, 256], P('pool', 'head', 'ctx')
- attn_out: bfloat16 [2, 512, 8192], P('pool', 'ctx', 'head')
The draws below stay inside these ranges and needn't reach their ends.
Inputs may be any that keep to these rules, and one draw needn't show every extreme that they name: `block_owner`: in each row c, every session owns exactly 32 slots, and each aligned run of 32 slots (one pool shard) holds at most 32 blocks of any one session; in every row some shard holds exactly 32 blocks of some session. `block_index`: in each row, the slots of one session carry the indices 0 to 31, each once. `history_len`: some session has exactly 4096. `turn_len`: every value is at least 256 and some session has exactly 512. `step_size`: Positive. `decay_rate`: Positive.
All inputs are finite; a program needn't handle non-finite values.
Results may differ from the reference program's by a relative error of at most 0.008.
Values may be sent and summed in bfloat16 or wider, within the bound.
No kernel may reach another device: no remote copies, remote signals or barrier semaphores. Data moves between devices by JAX's collectives and lax.ppermute only.
A program may use at most 64 MiB of HBM per device.

```python
import jax
import jax.numpy as jnp
from jax import lax

SSM_HEADS = 128
HEAD_P = 64
STATE = 256
GROUPS = 8
Q_HEADS = 64
KV_HEADS = 8
HEAD_DIM = 128
PAGE = 32
BLK = 128
REPLY_STEP_COUNT = 512
SESS = 2
SEGS = 4
HPAGES = 32
SLOTS = 64
HIST = 4096
N_HEAD = 4


def route_tables(key):
    start_shift = jax.random.fold_in(key, 7)
    per_pair = HPAGES // SESS

    def one_segment(seg_key):
        key_order, key_delta, key_shuffle, key_place = jax.random.split(seg_key, 4)
        order = jax.random.permutation(key_order, SESS)
        delta = jax.random.randint(key_delta, (SESS // 2,), 0, per_pair + 1).at[0].set(per_pair)
        counts = jnp.full((SESS,), per_pair, jnp.int32).at[order[0::2]].add(delta).at[order[1::2]].add(-delta)
        source = jnp.arange(SESS, dtype=jnp.int32)
        table = counts[(source[:, None] - source[None, :]) % SESS]
        edges = jnp.cumsum(table, axis=1)
        slot_ids = jnp.arange(HPAGES, dtype=jnp.int32)
        owner_seq = jnp.sum((slot_ids[None, :, None] >= edges[:, None, :]).astype(jnp.int32), axis=2)
        shuffles = jax.vmap(lambda one_key: jax.random.permutation(one_key, HPAGES))(jax.random.split(key_shuffle, SESS))
        owners = jnp.zeros((SESS, HPAGES), jnp.int32).at[source[:, None], shuffles].set(owner_seq)
        flat = owners.reshape(-1)
        onehot = (flat[:, None] == source[None, :]).astype(jnp.int32)
        order_in = jnp.sum((jnp.cumsum(onehot, axis=0) - onehot) * onehot, axis=1)
        places = jax.vmap(lambda one_key: jax.random.permutation(one_key, HPAGES))(jax.random.split(key_place, SESS))
        return (flat.astype(jnp.int32), places[flat, order_in].astype(jnp.int32))
    return jax.vmap(one_segment)(jax.random.split(start_shift, SEGS))


def draw_block_owner(key, part):
    return route_tables(key)[0]


def draw_block_index(key, part):
    return route_tables(key)[1]


def draw_history_len(key, part):
    key_len, key_top = jax.random.split(jax.random.fold_in(key, 3))
    lengths = jax.random.randint(key_len, (SESS,), 1, HIST + 1)
    chosen = jax.random.randint(key_top, (), 0, SESS)
    return lengths.at[chosen].set(HIST).astype(jnp.int32)


def draw_turn_len(key, part):
    key_len, key_top = jax.random.split(jax.random.fold_in(key, 5))
    lengths = jax.random.randint(key_len, (SESS,), REPLY_STEP_COUNT // 2, REPLY_STEP_COUNT + 1)
    chosen = jax.random.randint(key_top, (), 0, SESS)
    return lengths.at[chosen].set(REPLY_STEP_COUNT).astype(jnp.int32)


def draw_step_size(key, part):
    key_base, key_spot, key_level = jax.random.split(jax.random.fold_in(key, 9), 3)
    shape = (SESS, SSM_HEADS, REPLY_STEP_COUNT)
    start_shift = jnp.exp(jax.random.uniform(key_base, shape, jnp.float32, jnp.log(0.005), jnp.log(0.02)))
    cell_places = jax.random.randint(key_spot, (SESS, 1, 3), 0, REPLY_STEP_COUNT)
    spike_spot = jnp.any(jnp.arange(REPLY_STEP_COUNT, dtype=jnp.int32)[None, None, :, None] == cell_places[:, :, None, :], axis=3)
    height_amount = jax.random.uniform(key_level, (SESS, 1, REPLY_STEP_COUNT), jnp.float32, 1.0, 2.0)
    return jnp.where(spike_spot, height_amount, start_shift).astype(jnp.float32)


def draw_decay_rate(key, part):
    key_kind, key_slow, key_fast = jax.random.split(jax.random.fold_in(key, 13), 3)
    quick = jax.random.randint(key_kind, (SSM_HEADS,), 0, 2) == 0
    slow = jax.random.uniform(key_slow, (SSM_HEADS,), jnp.float32, 15.0 / REPLY_STEP_COUNT, 75.0 / REPLY_STEP_COUNT)
    fast = jax.random.uniform(key_fast, (SSM_HEADS,), jnp.float32, 2.0, 4.0)
    return jnp.where(quick, fast, slow).astype(jnp.float32)


def attention_pair(key):
    key_query, key_kv = jax.random.split(jax.random.fold_in(key, 17))
    width = KV_HEADS * HEAD_DIM
    turn = jnp.clip(jax.random.normal(key_kv, (SESS, 2, REPLY_STEP_COUNT, width), jnp.float32), -6.0, 6.0)
    asked = jnp.clip(jax.random.normal(key_query, (SESS, REPLY_STEP_COUNT, Q_HEADS * HEAD_DIM), jnp.float32), -6.0, 6.0)
    return (asked, turn)


def draw_queries(key, part):
    return attention_pair(key)[0].astype(jnp.bfloat16)


def draw_turn_kv(key, part):
    return attention_pair(key)[1].astype(jnp.bfloat16)


def block_scale(key, dims, shards, low, largest):
    loudness, own = 1.0, jax.random.fold_in(key, 6)
    for dim, shards_of in shards:
        steps = jnp.exp(jax.random.uniform(jax.random.fold_in(own, dim), (shards_of,), jnp.float32, low / len(shards), largest / len(shards)))
        loudness = loudness * jnp.repeat(steps, dims[dim] // shards_of).reshape([-1 if axis == dim else 1 for axis in range(len(dims))])
    return loudness


def bell_draw(stream_key, shape, scale, reach, pieces=(), kind=jnp.bfloat16):
    gain = block_scale(stream_key, shape, pieces, -0.22, 0.18) if pieces else 1.0
    drawn = jax.random.normal(stream_key, shape, jnp.float32) * scale * gain
    return jnp.minimum(jnp.maximum(drawn, -reach), reach).astype(kind)


def setup_inputs(seed: int = 0) -> dict:
    key_of = jax.random.split(jax.random.key(seed), 15)
    kv_pool = bell_draw(key_of[0], (SEGS, SLOTS, 2, PAGE, KV_HEADS * HEAD_DIM), 1.0, 6.0, ((0, 4), (1, 2), (4, 4)))
    state_pool = bell_draw(key_of[1], (SLOTS, HEAD_P, N_HEAD * STATE), 0.1, 0.59765625, ((0, 2), (1, 4), (2, 4)))
    block_owner = draw_block_owner(jax.random.fold_in(key_of[14], 71), 0)
    block_index = draw_block_index(jax.random.fold_in(key_of[14], 71), 0)
    history_len = draw_history_len(jax.random.fold_in(key_of[14], 71), 0)
    turn_len = draw_turn_len(jax.random.fold_in(key_of[14], 71), 0)
    mixer_in = bell_draw(key_of[6], (SESS, SSM_HEADS, HEAD_P, REPLY_STEP_COUNT), 1.0, 6.0, ((0, 2), (1, 4), (2, 4)))
    input_proj = bell_draw(key_of[7], (SESS, GROUPS, STATE, REPLY_STEP_COUNT), 0.25, 1.5, ((0, 2), (1, 4)))
    output_proj = bell_draw(key_of[8], (SESS, GROUPS, STATE, REPLY_STEP_COUNT), 1.0, 6.0, ((0, 2), (1, 4)))
    step_size = draw_step_size(jax.random.fold_in(key_of[14], 71), 0)
    decay_rate = draw_decay_rate(jax.random.fold_in(key_of[14], 71), 0)
    bypass_factor = jnp.clip(0.5 + 1.0 * jax.random.uniform(key_of[11], (SSM_HEADS,), jnp.float32) ** block_scale(key_of[11], (SSM_HEADS,), ((0, 4),), -0.2, 0.2), 0.5, 1.5)
    queries = draw_queries(jax.random.fold_in(key_of[14], 71), 0)
    turn_kv = draw_turn_kv(jax.random.fold_in(key_of[14], 71), 0)
    return {"kv_pool": kv_pool, "state_pool": state_pool, "block_owner": block_owner, "block_index": block_index, "history_len": history_len, "turn_len": turn_len, "mixer_in": mixer_in, "input_proj": input_proj, "output_proj": output_proj, "step_size": step_size, "decay_rate": decay_rate, "bypass_factor": bypass_factor, "queries": queries, "turn_kv": turn_kv}


floor_score = -1e30


def spanned_ssd(values, input_proj, output_proj, step_sizes, rates, bypass_factor, start_state, valid_len):
    heads, channels, total = values.shape
    groups = input_proj.shape[0]
    per_group = heads // groups
    count = total // BLK
    positions = jnp.arange(total, dtype=jnp.int32)
    live = positions < valid_len
    step_sizes = jnp.where(live[None, :], step_sizes, jnp.float32(0.0))
    value_blocks = values.reshape(heads, channels, count, BLK).transpose(2, 0, 1, 3)
    input_blocks = input_proj.reshape(groups, -1, count, BLK).transpose(2, 0, 1, 3)
    output_blocks = output_proj.reshape(groups, -1, count, BLK).transpose(2, 0, 1, 3)
    step_blocks = step_sizes.reshape(heads, count, BLK).transpose(1, 0, 2)
    offsets = jnp.arange(BLK, dtype=jnp.int32)
    lower = offsets[:, None] >= offsets[None, :]
    exact = lax.Precision.HIGHEST

    def advance(carried, item):
        value_blk, input_blk, output_blk, step_blk = item
        value_blk = value_blk.astype(jnp.float32)
        input_blk = input_blk.astype(jnp.float32)
        output_blk = output_blk.astype(jnp.float32)
        running = jnp.cumsum(-rates[:, None] * step_blk, axis=1)
        pairs = jnp.einsum("gnt,gns->gts", output_blk, input_blk, precision=exact)
        pairs = jnp.repeat(pairs, per_group, axis=0)
        gaps = jnp.minimum(running[:, :, None] - running[:, None, :], 0.0)
        mixing = jnp.where(lower[None], jnp.exp(gaps), 0.0) * pairs * step_blk[:, None, :]
        result = jnp.einsum("hts,hps->hpt", mixing, value_blk, precision=exact)
        read_out = jnp.repeat(output_blk, per_group, axis=0)
        result = result + jnp.exp(running)[:, None, :] * jnp.einsum("hpn,hnt->hpt", carried, read_out, precision=exact)
        result = result + bypass_factor[:, None, None] * value_blk
        weights = jnp.exp(running[:, -1:] - running) * step_blk
        write_in = jnp.repeat(input_blk, per_group, axis=0)
        carried = jnp.exp(running[:, -1])[:, None, None] * carried + jnp.einsum("hps,hns->hpn", value_blk * weights[:, None, :], write_in, precision=exact)
        return carried, result

    final_state, results = lax.scan(advance, start_state, (value_blocks, input_blocks, output_blocks, step_blocks))
    results = results.transpose(1, 2, 0, 3).reshape(heads, channels, total)
    return jnp.where(live[None, None, :], results, 0.0), final_state


def session_attention(item):
    query_rows, history, turn_kv, history_len, turn_len = item
    per_group = Q_HEADS // KV_HEADS
    keys_all = jnp.concatenate([history[0], turn_kv[0]], axis=0)
    values_all = jnp.concatenate([history[1], turn_kv[1]], axis=0)
    positions = jnp.arange(HIST + REPLY_STEP_COUNT, dtype=jnp.int32)
    in_history = positions < HIST
    turn_index = jnp.arange(REPLY_STEP_COUNT, dtype=jnp.int32)
    seen_mask = jnp.where(in_history[None, :], (positions < history_len)[None, :], (positions - HIST)[None, :] <= turn_index[:, None])
    query_heads = query_rows.reshape(REPLY_STEP_COUNT, KV_HEADS, per_group, HEAD_DIM).transpose(1, 0, 2, 3)
    key_heads = keys_all.reshape(HIST + REPLY_STEP_COUNT, KV_HEADS, HEAD_DIM).transpose(1, 0, 2)
    value_heads = values_all.reshape(HIST + REPLY_STEP_COUNT, KV_HEADS, HEAD_DIM).transpose(1, 0, 2)
    score_scale = HEAD_DIM ** -0.5

    def one_group(group_member):
        query_grp, key_grp, value_grp = group_member
        scores = jnp.einsum("tqd,kd->tqk", query_grp.astype(jnp.float32), key_grp.astype(jnp.float32), precision=lax.Precision.HIGHEST) * score_scale
        mask = seen_mask[:, None, :]
        top = jnp.max(jnp.where(mask, scores, floor_score), axis=-1, keepdims=True)
        weights = jnp.where(mask, jnp.exp(scores - top), 0.0)
        totals = jnp.sum(weights, axis=-1, keepdims=True)
        rounded = lax.optimization_barrier(weights.astype(jnp.bfloat16)).astype(jnp.float32)
        mixed = jnp.einsum("tqk,kd->tqd", rounded, value_grp.astype(jnp.float32), precision=lax.Precision.HIGHEST)
        return mixed / totals

    outputs = lax.map(one_group, (query_heads, key_heads, value_heads))
    outputs = outputs.transpose(1, 0, 2, 3).reshape(REPLY_STEP_COUNT, Q_HEADS * HEAD_DIM)
    return jnp.where((turn_index < turn_len)[:, None], outputs, 0.0).astype(jnp.bfloat16)


def reference(kv_pool, state_pool, block_owner, block_index, history_len, turn_len, mixer_in, input_proj, output_proj, step_size, decay_rate, bypass_factor, queries, turn_kv):
    width = KV_HEADS * HEAD_DIM
    page_ids = (block_owner * (SEGS * HPAGES) + jnp.arange(SEGS, dtype=jnp.int32)[:, None] * HPAGES + block_index).reshape(-1).astype(jnp.int32)
    pages = jnp.zeros((SESS * SEGS * HPAGES, 2, PAGE, width), kv_pool.dtype).at[page_ids].set(kv_pool.reshape(SEGS * SLOTS, 2, PAGE, width))
    history = pages.reshape(SESS, SEGS * HPAGES, 2, PAGE, width).transpose(0, 2, 1, 3, 4).reshape(SESS, 2, HIST, width)
    seg_chan = HEAD_P // SEGS
    blocks = state_pool.reshape(SLOTS, SEGS, seg_chan, N_HEAD, STATE).transpose(1, 0, 2, 3, 4)

    def place(owners, entry_numbers, slabs):
        return jnp.zeros((SESS, HPAGES, seg_chan, N_HEAD, STATE), state_pool.dtype).at[owners, entry_numbers].set(slabs)

    saved = jax.vmap(place)(block_owner, block_index, blocks)
    saved = saved.transpose(1, 4, 2, 0, 3, 5).reshape(SESS, SSM_HEADS, HEAD_P, STATE).astype(jnp.float32)

    def mamba_one(item):
        values, inputs, outputs, steps, start, valid = item
        return spanned_ssd(values, inputs, outputs, steps, decay_rate, bypass_factor, start, valid)

    mixed, final = lax.map(mamba_one, (mixer_in, input_proj, output_proj, step_size, saved, turn_len))
    attended = lax.map(session_attention, (queries, history, turn_kv, history_len, turn_len))
    return mixed.astype(jnp.bfloat16), final, attended
```

```python
import functools

import jax
import jax.numpy as jnp
from jax import lax
from jax.experimental import pallas as pl
from jax.experimental.pallas import tpu as pltpu
from jax.sharding import PartitionSpec as P

Q_HEADS = 64
KV_HEADS = 8
HEAD_DIM = 128
PER_GROUP = Q_HEADS // KV_HEADS
BLK = 128
HIDDEN = -1e30
TO_POWER = (HEAD_DIM**-0.5) * 1.4426950408889634
STAT_ROWS = 32
VMEM_BYTES = 56 * 2**20

whole = pl.BlockSpec(memory_space=pltpu.VMEM)
scalar = pl.BlockSpec(memory_space=pltpu.SMEM)
outside = pl.BlockSpec(memory_space=pl.ANY)


def params():
    return pltpu.CompilerParams(vmem_limit_bytes=VMEM_BYTES)


def mixer_kernel(valid_ref, x_ref, b_ref, c_ref, dt_ref, rate_ref, gain_ref, y_ref, s_ref, run_ref):
    heads, chans, total = x_ref.shape
    states = b_ref.shape[1]
    rows = heads * chans
    place = lax.broadcasted_iota(jnp.int32, (heads, total), 1)
    steps = jnp.where(place < valid_ref[0], dt_ref[...], 0.0)
    falls = -rate_ref[...] * steps
    gains = gain_ref[...]
    first = lax.broadcasted_iota(jnp.int32, (BLK, BLK), 0)
    second = lax.broadcasted_iota(jnp.int32, (BLK, BLK), 1)
    upper = first <= second
    ones_upper = jnp.where(upper, 1.0, 0.0).astype(jnp.float32)
    turned = b_ref[0].T
    state = jnp.zeros((rows, states), jnp.float32)
    base = jnp.zeros((heads, 1), jnp.float32)
    for blk in range(total // BLK):
        span = slice(blk * BLK, (blk + 1) * BLK)
        run = jnp.dot(
            falls[:, span],
            ones_upper,
            precision=lax.Precision.HIGHEST,
            preferred_element_type=jnp.float32,
        )
        run_col = run.T
        last = run[:, BLK - 1 :]
        pairs = jnp.dot(turned[span], c_ref[0, :, span], preferred_element_type=jnp.float32)
        pairs = jnp.where(upper, pairs, 0.0)
        x_blk = x_ref[:, :, span].astype(jnp.float32)
        stepped = (x_blk * steps[:, None, span]).astype(jnp.bfloat16)
        inside = []
        for head in range(heads):
            gap = jnp.minimum(run[head : head + 1, :] - run_col[:, head : head + 1], 0.0)
            mixing = (jnp.exp(gap) * pairs).astype(jnp.bfloat16)
            inside.append(jnp.dot(stepped[head], mixing, preferred_element_type=jnp.float32))
        result = jnp.stack(inside) + gains[:, :, None] * x_blk
        if blk:
            read = jnp.dot(
                state.astype(jnp.bfloat16), c_ref[0, :, span], preferred_element_type=jnp.float32
            )
            result = result + jnp.exp(run)[:, None, :] * read.reshape(heads, chans, BLK)
        y_ref[:, :, span] = result
        weights = jnp.exp(last - run) * steps[:, span]
        weighted = (x_blk * weights[:, None, :]).astype(jnp.bfloat16).reshape(rows, BLK)
        added = jnp.dot(weighted, turned[span], preferred_element_type=jnp.float32)
        kept = jnp.broadcast_to(jnp.exp(last)[:, :, None], (heads, chans, 1)).reshape(rows, 1)
        state = kept * state + added
        run_ref[:, span] = base + run
        base = base + last
    s_ref[...] = state.reshape(heads, chans, states)


def mixer_from_zero(x, b, c, dt, rates, gains, valid):
    heads, chans, total = x.shape
    groups, states, _ = b.shape
    per = heads // groups
    return pl.pallas_call(
        mixer_kernel,
        grid=(groups,),
        in_specs=[
            scalar,
            pl.BlockSpec((per, chans, total), lambda g: (g, 0, 0)),
            pl.BlockSpec((1, states, total), lambda g: (g, 0, 0)),
            pl.BlockSpec((1, states, total), lambda g: (g, 0, 0)),
            pl.BlockSpec((per, total), lambda g: (g, 0)),
            pl.BlockSpec((per, 1), lambda g: (g, 0)),
            pl.BlockSpec((per, 1), lambda g: (g, 0)),
        ],
        out_specs=[
            pl.BlockSpec((per, chans, total), lambda g: (g, 0, 0)),
            pl.BlockSpec((per, chans, states), lambda g: (g, 0, 0)),
            pl.BlockSpec((per, total), lambda g: (g, 0)),
        ],
        out_shape=[
            jax.ShapeDtypeStruct((heads, chans, total), jnp.float32),
            jax.ShapeDtypeStruct((heads, chans, states), jnp.float32),
            jax.ShapeDtypeStruct((heads, total), jnp.float32),
        ],
        compiler_params=params(),
        cost_estimate=pl.CostEstimate(
            flops=10**9, bytes_accessed=6 * 2**20, transcendentals=heads * total * BLK
        ),
        name="mixer_from_zero",
    )(valid, x, b, c, dt, rates[:, None], gains[:, None])


def saved_kernel(kinds, info_ref, *refs):
    slabs = refs[:kinds]
    y_ref, s_ref, run_ref, c_ref, out_ref, final_ref, start = refs[kinds:]
    heads, chans, total = y_ref.shape
    groups, states, _ = c_ref.shape
    per = heads // groups
    for kind in range(kinds):

        @pl.when(info_ref[0] == kind)
        def _():
            for slot in range(heads):
                start[info_ref[2 + slot]] = slabs[kind][slot]

    live = lax.broadcasted_iota(jnp.int32, (1, 1, total), 2) < info_ref[1]
    for group in range(groups):
        mine = slice(group * per, (group + 1) * per)
        saved = start[mine]
        fade = jnp.exp(run_ref[mine, :])
        read = jnp.dot(
            saved.reshape(per * chans, states), c_ref[group], preferred_element_type=jnp.float32
        ).reshape(per, chans, total)
        result = y_ref[mine] + fade[:, None, :] * read
        out_ref[mine] = jnp.where(live, result, 0.0).astype(jnp.bfloat16)
        kept = fade[:, None, total - 1 :]
        final_ref[mine] = s_ref[mine] + kept * saved.astype(jnp.float32)


def add_saved(slabs, kind, order, y, s, run, c, valid):
    heads, chans, total = y.shape
    states = c.shape[1]
    info = jnp.concatenate([kind[None], valid, order]).astype(jnp.int32)
    return pl.pallas_call(
        functools.partial(saved_kernel, len(slabs)),
        in_specs=[scalar] + [whole] * (len(slabs) + 4),
        out_specs=[whole, whole],
        out_shape=[
            jax.ShapeDtypeStruct((heads, chans, total), jnp.bfloat16),
            jax.ShapeDtypeStruct((heads, chans, states), jnp.float32),
        ],
        scratch_shapes=[pltpu.VMEM((heads, chans, states), jnp.bfloat16)],
        compiler_params=params(),
        cost_estimate=pl.CostEstimate(
            flops=10**8, bytes_accessed=5 * 2**20, transcendentals=heads * total
        ),
        name="add_saved",
    )(info, *slabs, y, s, run, c)


def attend_kernel(kinds, head, info_ref, *refs):
    q_refs = refs[:2]
    kv_refs = (refs[2 : 2 + kinds], refs[2 + kinds : 2 + 2 * kinds])
    turn_refs = refs[2 + 2 * kinds : 4 + 2 * kinds]
    o_ref, l_ref, sent_ref, queries, keys, turn_keys, turn_raw, values, sems = refs[
        4 + 2 * kinds :
    ]
    pages, page = kv_refs[0][0].shape[0], kv_refs[0][0].shape[2]
    rows = q_refs[0].shape[0]
    history = pages * page
    width = PER_GROUP * HEAD_DIM
    columns = pl.ds(head * HEAD_DIM, HEAD_DIM)
    copies = []
    for side in range(2):
        copies.append(
            pltpu.make_async_copy(
                q_refs[side].at[:, pl.ds(head * width, width)], queries.at[side], sems.at[side]
            )
        )
        copies.append(
            pltpu.make_async_copy(
                turn_refs[side].at[:, :, columns], turn_raw.at[side], sems.at[2 + side]
            )
        )
    for copy in copies:
        copy.start()
    slot = [2 + side * (2 + pages) for side in range(2)]
    base = [1 + side * (2 + pages) for side in range(2)]
    for side in range(2):
        for kind in range(kinds):

            @pl.when(info_ref[base[side] + 1] == kind)
            def _():
                pltpu.make_async_copy(
                    kv_refs[side][kind].at[:, 0],
                    keys.at[pl.ds(side * pages, pages), :, pl.ds(0, HEAD_DIM)],
                    sems.at[4 + side],
                ).start()
                pltpu.make_async_copy(
                    kv_refs[side][kind].at[:, 1],
                    values.at[pl.ds(side * pages, pages), :, pl.ds(0, HEAD_DIM)],
                    sems.at[6 + side],
                ).start()

    in_page = lax.broadcasted_iota(jnp.int32, (page, HEAD_DIM), 0)
    seen = info_ref[0]
    for side in range(2):
        start = info_ref[base[side]] * history
        for number in range(pages):
            left = seen - start - info_ref[base[side] + 2 + number] * page
            keys[side * pages + number, :, HEAD_DIM:] = jnp.where(
                in_page < left, 0.0, HIDDEN
            ).astype(jnp.bfloat16)
    values[:, :, HEAD_DIM:] = jnp.ones(
        (values.shape[0], page, HEAD_DIM), jnp.bfloat16
    )
    first = lax.broadcasted_iota(jnp.int32, (rows, rows), 0)
    second = lax.broadcasted_iota(jnp.int32, (rows, rows), 1)
    eye = jnp.where(first == second, 1.0, 0.0).astype(jnp.bfloat16)
    asking = (info_ref[base[0]], info_ref[base[0]] ^ 2)
    for asked in range(2):
        for side in range(2):
            ahead = first + info_ref[base[side]] * rows
            turn_keys[asked, pl.ds(side * rows, rows), HEAD_DIM:] = jnp.where(
                ahead <= second + asking[asked] * rows, 0.0, HIDDEN
            ).astype(jnp.bfloat16)
    for copy in copies:
        copy.wait()
    turn_pages = rows // page
    for side in range(2):
        for asked in range(2):
            turn_keys[asked, pl.ds(side * rows, rows), pl.ds(0, HEAD_DIM)] = turn_raw[side, 0]
        values[
            pl.ds(2 * pages + side * turn_pages, turn_pages), :, pl.ds(0, HEAD_DIM)
        ] = turn_raw[side, 1].reshape(turn_pages, page, HEAD_DIM)
    for side in range(2):
        pltpu.make_async_copy(
            kv_refs[side][0].at[:, 0],
            keys.at[pl.ds(side * pages, pages), :, pl.ds(0, HEAD_DIM)],
            sems.at[4 + side],
        ).wait()
        pltpu.make_async_copy(
            kv_refs[side][0].at[:, 1],
            values.at[pl.ds(side * pages, pages), :, pl.ds(0, HEAD_DIM)],
            sems.at[6 + side],
        ).wait()
    depth = 2 * HEAD_DIM
    all_keys = 2 * history
    lane = lax.broadcasted_iota(jnp.int32, (rows, HEAD_DIM), 1)
    across = (((1,), (1,)), ((), ()))
    at_once = 2
    for asked in (1, 0):
        stats = jnp.zeros((rows, HEAD_DIM), jnp.float32)
        for batch in range(PER_GROUP // at_once):
            asks = jnp.concatenate(
                [
                    jnp.concatenate(
                        [
                            queries[asked, :, pl.ds((batch * at_once + i) * HEAD_DIM, HEAD_DIM)],
                            eye,
                        ],
                        axis=1,
                    )
                    for i in range(at_once)
                ],
                axis=0,
            )
            scores = jnp.concatenate(
                [
                    lax.dot_general(
                        asks,
                        keys[...].reshape(all_keys, depth),
                        across,
                        preferred_element_type=jnp.float32,
                    ),
                    lax.dot_general(
                        asks, turn_keys[asked], across, preferred_element_type=jnp.float32
                    ),
                ],
                axis=1,
            )
            peak = jnp.max(scores, axis=1, keepdims=True)
            weights = jnp.exp2((scores - peak) * TO_POWER).astype(jnp.bfloat16)
            summed = jnp.dot(
                weights,
                values[...].reshape(all_keys + 2 * rows, depth),
                preferred_element_type=jnp.float32,
            )
            totals = summed[:, HEAD_DIM:]
            mixed = (summed[:, :HEAD_DIM] / totals).astype(jnp.bfloat16)
            level = peak * TO_POWER + jnp.log2(totals)
            span = pl.ds(batch * at_once * rows, at_once * rows)
            if asked:
                sent_ref[span] = mixed
            else:
                o_ref[span] = mixed
            for i in range(at_once):
                stats = jnp.where(
                    lane == batch * at_once + i, level[i * rows : (i + 1) * rows], stats
                )
        stats = stats.T[:PER_GROUP]
        if asked:
            high = stats.astype(jnp.bfloat16).astype(jnp.float32)
            middle = (stats - high).astype(jnp.bfloat16).astype(jnp.float32)
            low = stats - high - middle
            sent_ref[pl.ds(PER_GROUP * rows, STAT_ROWS)] = jnp.concatenate(
                [high, middle, low, jnp.zeros_like(low)], axis=0
            ).astype(jnp.bfloat16)
        else:
            l_ref[...] = stats


def attend(head, info, queries, own_kv, partner_kv, turns):
    rows = queries[0].shape[0]
    pages, _, page, _ = own_kv[0].shape
    kinds = len(own_kv)
    all_rows = PER_GROUP * rows
    return pl.pallas_call(
        functools.partial(attend_kernel, kinds, head),
        in_specs=[scalar] + [outside] * (4 + 2 * kinds),
        out_specs=[whole] * 3,
        out_shape=[
            jax.ShapeDtypeStruct((all_rows, HEAD_DIM), jnp.bfloat16),
            jax.ShapeDtypeStruct((PER_GROUP, rows), jnp.float32),
            jax.ShapeDtypeStruct((all_rows + STAT_ROWS, HEAD_DIM), jnp.bfloat16),
        ],
        scratch_shapes=[
            pltpu.VMEM((2, rows, PER_GROUP * HEAD_DIM), jnp.bfloat16),
            pltpu.VMEM((2 * pages, page, 2 * HEAD_DIM), jnp.bfloat16),
            pltpu.VMEM((2, 2 * rows, 2 * HEAD_DIM), jnp.bfloat16),
            pltpu.VMEM((2, 2, rows, HEAD_DIM), jnp.bfloat16),
            pltpu.VMEM((2 * pages + 2 * rows // page, page, 2 * HEAD_DIM), jnp.bfloat16),
            pltpu.SemaphoreType.DMA((8,)),
        ],
        compiler_params=params(),
        cost_estimate=pl.CostEstimate(
            flops=8 * all_rows * 2 * pages * page * HEAD_DIM,
            bytes_accessed=3 * 2**20,
            transcendentals=4 * all_rows * pages * page,
        ),
        name=f"attend_{head}",
    )(info, *queries, *own_kv, *partner_kv, *turns)


def merge_kernel(heads, info_ref, *refs):
    out_ref = refs[-1]
    rows = out_ref.shape[0]
    live = lax.broadcasted_iota(jnp.int32, (rows, HEAD_DIM), 0) < info_ref[0]
    for head in range(heads):
        o_ref, l_ref, got_ref = refs[3 * head : 3 * head + 3]
        parts = got_ref[pl.ds(PER_GROUP * rows, STAT_ROWS)].astype(jnp.float32)
        level = parts[:PER_GROUP] + parts[PER_GROUP : 2 * PER_GROUP]
        level = level + parts[2 * PER_GROUP : 3 * PER_GROUP]
        share = 1.0 / (1.0 + jnp.exp2(level - l_ref[...]))
        share = jnp.concatenate(
            [share, jnp.zeros((rows - PER_GROUP, rows), jnp.float32)], axis=0
        ).T
        for member in range(PER_GROUP):
            span = pl.ds(member * rows, rows)
            here = o_ref[span].astype(jnp.float32)
            there = got_ref[span].astype(jnp.float32)
            result = there + share[:, member : member + 1] * (here - there)
            out_ref[:, pl.ds((head * PER_GROUP + member) * HEAD_DIM, HEAD_DIM)] = jnp.where(
                live, result, 0.0
            ).astype(jnp.bfloat16)


def merge(parts, live, rows):
    heads = len(parts)
    flat = [array for part in parts for array in part]
    return pl.pallas_call(
        functools.partial(merge_kernel, heads),
        in_specs=[scalar] + [whole] * len(flat),
        out_specs=whole,
        out_shape=jax.ShapeDtypeStruct((rows, heads * PER_GROUP * HEAD_DIM), jnp.bfloat16),
        compiler_params=params(),
        name="merge",
    )(live, *flat)


def route_blocks(kv_local, state_local, owner_row, index_row):
    parties = lax.axis_size("pool")
    myself = lax.axis_index("pool")
    pages = kv_local.shape[0]
    capacity = max(1, 2 * pages // parties)
    sessions = jnp.arange(parties, dtype=jnp.int32)
    table = (
        (owner_row[:, None] == sessions[None, :]).astype(jnp.int32).reshape(parties, pages, parties)
    )
    before = jnp.cumsum(table, axis=1) - table
    ranks = jnp.sum(before * table, axis=2)
    owners = owner_row.reshape(parties, pages)
    my_owner = lax.dynamic_index_in_dim(owners, myself, 0, keepdims=False)
    device_rank = lax.dynamic_index_in_dim(ranks, myself, 0, keepdims=False)

    def spread(array):
        empty = jnp.zeros((parties, capacity) + array.shape[1:], array.dtype)
        sent = empty.at[my_owner, device_rank].set(array)
        return lax.all_to_all(sent, "pool", split_axis=0, concat_axis=0, tiled=True)

    got_kv, got_state = spread(kv_local), spread(state_local)
    flat_place = (sessions[:, None] * capacity + ranks).reshape(-1)
    target = jnp.where(owner_row == myself, index_row, pages)
    where_from = jnp.zeros((pages,), jnp.int32).at[target].set(flat_place, mode="drop")
    return (
        got_kv.reshape((parties * capacity,) + kv_local.shape[1:])[where_from],
        got_state.reshape((parties * capacity,) + state_local.shape[1:])[where_from],
    )


def local(
    kv_pool,
    state_pool,
    block_owner,
    block_index,
    history_len,
    turn_len,
    mixer_in,
    input_proj,
    output_proj,
    step_size,
    decay_rate,
    bypass_factor,
    queries,
    turn_kv,
):
    parties = lax.axis_size("pool")
    myself = lax.axis_index("pool")
    segment = lax.axis_index("ctx")
    segments = lax.axis_size("ctx")
    kv = kv_pool[0]
    pages = kv.shape[0]
    rows = queries.shape[1]
    heads = kv.shape[-1] // HEAD_DIM
    partner = [(i, i ^ 1) for i in range(segments)]
    opposite = [(i, i ^ 2) for i in range(segments)]

    def to_partner(array):
        return lax.ppermute(array, "ctx", partner)

    def to_opposite(array):
        return lax.ppermute(array, "ctx", opposite)

    owners, places = block_owner[0], block_index[0]
    if parties == 2:
        swap = [(0, 1), (1, 0)]
        kind = (lax.dynamic_index_in_dim(owners, myself * pages, 0, keepdims=False) != myself).astype(
            jnp.int32
        )
        order = lax.dynamic_slice_in_dim(places, jnp.where(kind == 0, myself, 1 - myself) * pages, pages)
        slices = [kv[..., h * HEAD_DIM : (h + 1) * HEAD_DIM] for h in range(heads)]
        own_kv = [(piece, lax.ppermute(piece, "pool", swap)) for piece in slices]
        slabs = (state_pool, lax.ppermute(state_pool, "pool", swap))
    else:
        kind = jnp.zeros((), jnp.int32)
        order = jnp.arange(pages, dtype=jnp.int32)
        routed, slab = route_blocks(kv, state_pool, owners, places)
        own_kv = [(routed[..., h * HEAD_DIM : (h + 1) * HEAD_DIM],) for h in range(heads)]
        slabs = (slab,)
    partner_kv = [tuple(to_partner(piece) for piece in choice) for choice in own_kv]
    turns = (turn_kv[0], to_partner(turn_kv[0]))
    asks = (queries[0], to_opposite(queries[0]))
    own_info = jnp.concatenate([segment[None].astype(jnp.int32), kind[None], order])
    info = jnp.concatenate([history_len, own_info, to_partner(own_info)]).astype(jnp.int32)

    y, s, run = mixer_from_zero(
        mixer_in[0], input_proj[0], output_proj[0], step_size[0], decay_rate, bypass_factor, turn_len
    )
    parts = []
    for head in range(heads):
        o, level, sent = attend(head, info, asks, own_kv[head], partner_kv[head], turns)
        parts.append((o, level, to_opposite(sent)))
    mixed, final = add_saved(slabs, kind, order, y, s, run, output_proj[0], turn_len)
    live = turn_len - segment.astype(jnp.int32) * rows
    attended = merge(parts, live, rows)
    return (mixed[None], final[None], attended[None])


def solution(mesh):
    return jax.shard_map(
        local,
        mesh=mesh,
        in_specs=(
            P("ctx", "pool", None, None, "head"),
            P("pool", "ctx", "head"),
            P("ctx", None),
            P("ctx", None),
            P("pool"),
            P("pool"),
            P("pool", "head", "ctx", None),
            P("pool", "head", None, None),
            P("pool", "head", None, None),
            P("pool", "head", None),
            P("head"),
            P("head"),
            P("pool", "ctx", "head"),
            P("pool", None, "ctx", "head"),
        ),
        out_specs=(
            P("pool", "head", "ctx", None),
            P("pool", "head", "ctx", None),
            P("pool", "ctx", "head"),
        ),
        check_vma=False,
    )
```

```python
import functools

import jax
import jax.numpy as jnp
from jax import lax
from jax.experimental import pallas as pl
from jax.experimental.pallas import tpu as pltpu
from jax.sharding import PartitionSpec as P

Q_HEADS = 64
KV_HEADS = 8
HEAD_DIM = 128
PER_GROUP = Q_HEADS // KV_HEADS
BLK = 128
HIDDEN = -1e30
TO_POWER = (HEAD_DIM**-0.5) * 1.4426950408889634
STAT_ROWS = 32

whole = pl.BlockSpec(memory_space=pltpu.VMEM)
scalar = pl.BlockSpec(memory_space=pltpu.SMEM)
outside = pl.BlockSpec(memory_space=pl.ANY)
distant = pl.BlockSpec(memory_space=pltpu.HBM)


def params(mib):
    return pltpu.CompilerParams(vmem_limit_bytes=mib * 2**20)


def locate(kinds, owner_ref, pages):
    if kinds == 1:
        return 0, 0
    myself = lax.axis_index("pool")
    kind = jnp.where(owner_ref[0, myself * pages] == myself, 0, 1).astype(jnp.int32)
    return kind, jnp.where(kind == 0, myself, 1 - myself) * pages


def as_column(row_ref, start, count):
    row = jnp.broadcast_to(row_ref[...], (count, row_ref.shape[1]))
    across = lax.broadcasted_iota(jnp.int32, row.shape, 1)
    down = lax.broadcasted_iota(jnp.int32, row.shape, 0)
    return jnp.sum(jnp.where(across == down + start, row, 0.0), axis=1, keepdims=True)


def mixer_kernel(valid_ref, x_ref, b_ref, c_ref, dt_ref, rate_ref, gain_ref, y_ref, s_ref, run_ref):
    heads, chans, total = x_ref.shape
    start = pl.program_id(0) * heads
    states = b_ref.shape[1]
    rows = heads * chans
    place = lax.broadcasted_iota(jnp.int32, (heads, total), 1)
    steps = jnp.where(place < valid_ref[0], dt_ref[...], 0.0)
    falls = -as_column(rate_ref, start, heads) * steps
    gains = as_column(gain_ref, start, heads)
    first = lax.broadcasted_iota(jnp.int32, (BLK, BLK), 0)
    second = lax.broadcasted_iota(jnp.int32, (BLK, BLK), 1)
    upper = first <= second
    ones_upper = jnp.where(upper, 1.0, 0.0).astype(jnp.float32)
    turned = b_ref[0].T
    state = jnp.zeros((rows, states), jnp.float32)
    base = jnp.zeros((heads, 1), jnp.float32)
    for blk in range(total // BLK):
        span = slice(blk * BLK, (blk + 1) * BLK)
        run = jnp.dot(
            falls[:, span],
            ones_upper,
            precision=lax.Precision.HIGHEST,
            preferred_element_type=jnp.float32,
        )
        run_col = run.T
        last = run[:, BLK - 1 :]
        pairs = jnp.dot(turned[span], c_ref[0, :, span], preferred_element_type=jnp.float32)
        pairs = jnp.where(upper, pairs, 0.0)
        x_blk = x_ref[:, :, span].astype(jnp.float32)
        stepped = (x_blk * steps[:, None, span]).astype(jnp.bfloat16)
        inside = []
        for head in range(heads):
            gap = jnp.minimum(run[head : head + 1, :] - run_col[:, head : head + 1], 0.0)
            mixing = (jnp.exp(gap) * pairs).astype(jnp.bfloat16)
            inside.append(jnp.dot(stepped[head], mixing, preferred_element_type=jnp.float32))
        result = jnp.stack(inside) + gains[:, :, None] * x_blk
        if blk:
            read = jnp.dot(
                state.astype(jnp.bfloat16), c_ref[0, :, span], preferred_element_type=jnp.float32
            )
            result = result + jnp.exp(run)[:, None, :] * read.reshape(heads, chans, BLK)
        y_ref[:, :, span] = result
        weights = jnp.exp(last - run) * steps[:, span]
        weighted = (x_blk * weights[:, None, :]).astype(jnp.bfloat16).reshape(rows, BLK)
        added = jnp.dot(weighted, turned[span], preferred_element_type=jnp.float32)
        kept = jnp.broadcast_to(jnp.exp(last)[:, :, None], (heads, chans, 1)).reshape(rows, 1)
        state = kept * state + added
        run_ref[:, span] = base + run
        base = base + last
    s_ref[...] = state.reshape(heads, chans, states)


def mixer_from_zero(valid, x, b, c, dt, rates, gains):
    heads, chans, total = x.shape
    groups, states, _ = b.shape
    per = heads // groups
    return pl.pallas_call(
        mixer_kernel,
        grid=(groups,),
        in_specs=[
            scalar,
            pl.BlockSpec((per, chans, total), lambda g: (g, 0, 0)),
            pl.BlockSpec((1, states, total), lambda g: (g, 0, 0)),
            pl.BlockSpec((1, states, total), lambda g: (g, 0, 0)),
            pl.BlockSpec((per, total), lambda g: (g, 0)),
            pl.BlockSpec((1, heads), lambda g: (0, 0)),
            pl.BlockSpec((1, heads), lambda g: (0, 0)),
        ],
        out_specs=[
            pl.BlockSpec((per, chans, total), lambda g: (g, 0, 0)),
            pl.BlockSpec((per, chans, states), lambda g: (g, 0, 0)),
            pl.BlockSpec((per, total), lambda g: (g, 0)),
        ],
        out_shape=[
            jax.ShapeDtypeStruct((heads, chans, total), jnp.float32),
            jax.ShapeDtypeStruct((heads, chans, states), jnp.float32),
            jax.ShapeDtypeStruct((heads, total), jnp.float32),
        ],
        compiler_params=params(16),
        cost_estimate=pl.CostEstimate(flops=1, bytes_accessed=1, transcendentals=0),
        name="mixer_from_zero",
    )(valid, x, b, c, dt, rates[None], gains[None])


def saved_kernel(kinds, valid_ref, owner_ref, place_ref, *refs):
    refs = refs[1:]
    slabs = refs[:kinds]
    y_ref, s_ref, run_ref, c_ref, out_ref, final_ref, done_ref, start, mixed, final, sems = refs[
        kinds:
    ]
    done_ref[...] = jnp.zeros(done_ref.shape, jnp.float32)
    heads, chans, total = y_ref.shape
    groups, states, _ = c_ref.shape
    per = heads // groups
    copies = []
    chosen, source = locate(kinds, owner_ref, heads)
    for kind in range(kinds):

        @pl.when(chosen == kind)
        def _():
            for slot in range(heads):
                start[place_ref[0, source + slot]] = slabs[kind][slot]

    live = lax.broadcasted_iota(jnp.int32, (1, 1, total), 2) < valid_ref[0]
    for group in range(groups):
        mine = slice(group * per, (group + 1) * per)
        saved = start[mine]
        fade = jnp.exp(run_ref[mine, :])
        read = jnp.dot(
            saved.reshape(per * chans, states), c_ref[group], preferred_element_type=jnp.float32
        ).reshape(per, chans, total)
        result = y_ref[mine] + fade[:, None, :] * read
        mixed[mine] = jnp.where(live, result, 0.0).astype(jnp.bfloat16)
        kept = fade[:, None, total - 1 :]
        final[mine] = s_ref[mine] + kept * saved.astype(jnp.float32)
        span = pl.ds(group * per, per)
        for held, target in ((mixed, out_ref), (final, final_ref)):
            copies.append(
                pltpu.make_async_copy(held.at[span], target.at[span], sems.at[len(copies)])
            )
            copies[-1].start()
    for copy in copies:
        copy.wait()


def add_saved(after, valid, rows, slabs, y, s, run, c):
    heads, chans, total = y.shape
    groups, states, _ = c.shape
    return pl.pallas_call(
        functools.partial(saved_kernel, len(slabs)),
        in_specs=[scalar] * 3 + [outside] + [whole] * (len(slabs) + 4),
        out_specs=[distant, distant, whole],
        out_shape=[
            jax.ShapeDtypeStruct((heads, chans, total), jnp.bfloat16),
            jax.ShapeDtypeStruct((heads, chans, states), jnp.float32),
            jax.ShapeDtypeStruct((8, 128), jnp.float32),
        ],
        scratch_shapes=[
            pltpu.VMEM((heads, chans, states), jnp.bfloat16),
            pltpu.VMEM((heads, chans, total), jnp.bfloat16),
            pltpu.VMEM((heads, chans, states), jnp.float32),
            pltpu.SemaphoreType.DMA((2 * groups,)),
        ],
        compiler_params=params(12),
        cost_estimate=pl.CostEstimate(flops=1, bytes_accessed=1, transcendentals=0),
        name="add_saved",
    )(valid, *rows, after, *slabs, y, s, run, c)


def attend_kernel(counts, head, sides, seen_ref, *refs):
    rows_refs, refs = (refs[0:2], refs[2:4]), refs[4:]
    refs = refs[1:]
    q_refs, turn_refs, refs = refs[: len(sides)], refs[len(sides) : len(sides) + 2], refs[len(sides) + 2 :]
    kinds = len(counts)
    kv_refs = ([], [])
    for side in range(2):
        for count in counts:
            kv_refs[side].append(refs[:count])
            refs = refs[count:]
    out_refs = {}
    for asked in sides:
        out_refs[asked], refs = refs[0], refs[1:]
        if asked == 0:
            l_ref, refs = refs[0], refs[1:]
    queries, keys, turn_keys, turn_raw, values, sems = refs
    pages, page = kv_refs[0][0][0].shape[0], kv_refs[0][0][0].shape[-2]
    rows = q_refs[0].shape[0]
    history = pages * page
    width = PER_GROUP * HEAD_DIM
    segment = lax.axis_index("ctx")
    numbers = (segment, segment ^ 1)
    found = [locate(kinds, rows_refs[side][0], pages) for side in range(2)]
    columns = pl.ds(head * HEAD_DIM, HEAD_DIM)
    copies = [
        pltpu.make_async_copy(q_ref.at[:, pl.ds(head * width, width)], queries.at[i], sems.at[i])
        for i, q_ref in enumerate(q_refs)
    ]
    for side in range(2):
        copies.append(
            pltpu.make_async_copy(
                turn_refs[side].at[:, :, columns], turn_raw.at[side], sems.at[2 + side]
            )
        )

    def page_copies(side, kind):
        sources = kv_refs[side][kind]
        if len(sources) == 1:
            sources = [sources[0].at[:, half] for half in range(2)]
        wide = sources[0].shape[2] > HEAD_DIM
        lanes = columns if wide else pl.ds(0, HEAD_DIM)
        target = pl.ds(side * pages, pages)
        return [
            pltpu.make_async_copy(
                sources[half].at[:, :, lanes],
                place.at[target, :, pl.ds(0, HEAD_DIM)],
                sems.at[4 + 2 * half + side],
            )
            for half, place in enumerate((keys, values))
        ]

    for side in range(2):
        for kind in range(kinds):

            @pl.when(found[side][0] == kind)
            def _():
                for copy in page_copies(side, kind):
                    copy.start()

    for copy in copies:
        copy.start()
    in_page = lax.broadcasted_iota(jnp.int32, (page, HEAD_DIM), 0)
    seen = seen_ref[0]
    for side in range(2):
        start = numbers[side] * history
        for number in range(pages):
            left = seen - start - rows_refs[side][1][0, found[side][1] + number] * page
            keys[side * pages + number, :, HEAD_DIM:] = jnp.where(
                in_page < left, 0.0, HIDDEN
            ).astype(jnp.bfloat16)
    values[:, :, HEAD_DIM:] = jnp.ones(
        (values.shape[0], page, HEAD_DIM), jnp.bfloat16
    )
    first = lax.broadcasted_iota(jnp.int32, (rows, rows), 0)
    second = lax.broadcasted_iota(jnp.int32, (rows, rows), 1)
    eye = jnp.where(first == second, 1.0, 0.0).astype(jnp.bfloat16)
    for i, asked in enumerate(sides):
        asking = segment ^ (2 * asked)
        for side in range(2):
            ahead = first + numbers[side] * rows
            turn_keys[i, pl.ds(side * rows, rows), HEAD_DIM:] = jnp.where(
                ahead <= second + asking * rows, 0.0, HIDDEN
            ).astype(jnp.bfloat16)
    for copy in copies:
        copy.wait()
    turn_pages = rows // page
    for side in range(2):
        for i in range(len(sides)):
            turn_keys[i, pl.ds(side * rows, rows), pl.ds(0, HEAD_DIM)] = turn_raw[side, 0]
        values[
            pl.ds(2 * pages + side * turn_pages, turn_pages), :, pl.ds(0, HEAD_DIM)
        ] = turn_raw[side, 1].reshape(turn_pages, page, HEAD_DIM)
    for side in range(2):
        for copy in page_copies(side, 0):
            copy.wait()
    depth = 2 * HEAD_DIM
    all_keys = 2 * history
    lane = lax.broadcasted_iota(jnp.int32, (rows, HEAD_DIM), 1)
    across = (((1,), (1,)), ((), ()))
    at_once = 2
    for which, asked in enumerate(sides):
        out_ref = out_refs[asked]
        stats = jnp.zeros((rows, HEAD_DIM), jnp.float32)
        for batch in range(PER_GROUP // at_once):
            asks = jnp.concatenate(
                [
                    jnp.concatenate(
                        [
                            queries[which, :, pl.ds((batch * at_once + i) * HEAD_DIM, HEAD_DIM)],
                            eye,
                        ],
                        axis=1,
                    )
                    for i in range(at_once)
                ],
                axis=0,
            )
            scores = jnp.concatenate(
                [
                    lax.dot_general(
                        asks,
                        keys[...].reshape(all_keys, depth),
                        across,
                        preferred_element_type=jnp.float32,
                    ),
                    lax.dot_general(
                        asks, turn_keys[which], across, preferred_element_type=jnp.float32
                    ),
                ],
                axis=1,
            )
            peak = jnp.max(scores, axis=1, keepdims=True)
            weights = jnp.exp2((scores - peak) * TO_POWER).astype(jnp.bfloat16)
            summed = jnp.dot(
                weights,
                values[...].reshape(all_keys + 2 * rows, depth),
                preferred_element_type=jnp.float32,
            )
            totals = summed[:, HEAD_DIM:]
            mixed = (summed[:, :HEAD_DIM] / totals).astype(jnp.bfloat16)
            level = peak * TO_POWER + jnp.log2(totals)
            span = pl.ds(batch * at_once * rows, at_once * rows)
            out_ref[span] = mixed
            for i in range(at_once):
                stats = jnp.where(
                    lane == batch * at_once + i, level[i * rows : (i + 1) * rows], stats
                )
        stats = stats.T[:PER_GROUP]
        if asked:
            high = stats.astype(jnp.bfloat16).astype(jnp.float32)
            middle = (stats - high).astype(jnp.bfloat16).astype(jnp.float32)
            low = stats - high - middle
            out_ref[pl.ds(PER_GROUP * rows, STAT_ROWS)] = jnp.concatenate(
                [high, middle, low, jnp.zeros_like(low)], axis=0
            ).astype(jnp.bfloat16)
        else:
            l_ref[...] = stats


def attend(head, sides, seen, tables, after, queries, own_kv, partner_kv, turns):
    rows = queries[0].shape[0]
    pages, page = own_kv[0][0].shape[0], own_kv[0][0].shape[-2]
    counts = tuple(len(choice) for choice in own_kv)
    flat = [array for choice in (*own_kv, *partner_kv) for array in choice]
    all_rows = PER_GROUP * rows
    shapes = []
    for asked in sides:
        extra = STAT_ROWS if asked else 0
        shapes.append(jax.ShapeDtypeStruct((all_rows + extra, HEAD_DIM), jnp.bfloat16))
        if not asked:
            shapes.append(jax.ShapeDtypeStruct((PER_GROUP, rows), jnp.float32))
    asks = [queries[asked] for asked in sides]
    return pl.pallas_call(
        functools.partial(attend_kernel, counts, head, sides),
        in_specs=[scalar] * 5 + [outside] * (3 + len(sides) + len(flat)),
        out_specs=[whole] * len(shapes),
        out_shape=shapes,
        scratch_shapes=[
            pltpu.VMEM((len(sides), rows, PER_GROUP * HEAD_DIM), jnp.bfloat16),
            pltpu.VMEM((2 * pages, page, 2 * HEAD_DIM), jnp.bfloat16),
            pltpu.VMEM((len(sides), 2 * rows, 2 * HEAD_DIM), jnp.bfloat16),
            pltpu.VMEM((2, 2, rows, HEAD_DIM), jnp.bfloat16),
            pltpu.VMEM((2 * pages + 2 * rows // page, page, 2 * HEAD_DIM), jnp.bfloat16),
            pltpu.SemaphoreType.DMA((8,)),
        ],
        compiler_params=params(24),
        cost_estimate=pl.CostEstimate(flops=1, bytes_accessed=1, transcendentals=0),
        name=f"attend_{head}_{len(sides)}_{sides[0]}",
    )(seen, *tables, after, *asks, *turns, *flat)


def merge_kernel(heads, valid_ref, *refs):
    refs = refs[1:]
    out_ref, held, sem = refs[-3:]
    rows = out_ref.shape[0]
    width = PER_GROUP * HEAD_DIM
    place = lax.axis_index("ctx") * rows + lax.broadcasted_iota(jnp.int32, (rows, HEAD_DIM), 0)
    live = place < valid_ref[0]
    copies = []
    for head in range(heads):
        o_ref, l_ref, got_ref = refs[3 * head : 3 * head + 3]
        parts = got_ref[pl.ds(PER_GROUP * rows, STAT_ROWS)].astype(jnp.float32)
        level = parts[:PER_GROUP] + parts[PER_GROUP : 2 * PER_GROUP]
        level = level + parts[2 * PER_GROUP : 3 * PER_GROUP]
        share = 1.0 / (1.0 + jnp.exp2(level - l_ref[...]))
        share = jnp.concatenate(
            [share, jnp.zeros((rows - PER_GROUP, rows), jnp.float32)], axis=0
        ).T
        for member in range(PER_GROUP):
            span = pl.ds(member * rows, rows)
            here = o_ref[span].astype(jnp.float32)
            there = got_ref[span].astype(jnp.float32)
            result = there + share[:, member : member + 1] * (here - there)
            held[:, pl.ds((head * PER_GROUP + member) * HEAD_DIM, HEAD_DIM)] = jnp.where(
                live, result, 0.0
            ).astype(jnp.bfloat16)
        lanes = pl.ds(head * width, width)
        copies.append(pltpu.make_async_copy(held.at[:, lanes], out_ref.at[:, lanes], sem.at[head]))
        copies[-1].start()
    for copy in copies:
        copy.wait()


def merge(after, valid, parts, rows):
    heads = len(parts)
    flat = [array for part in parts for array in part]
    shape = jax.ShapeDtypeStruct((rows, heads * PER_GROUP * HEAD_DIM), jnp.bfloat16)
    return pl.pallas_call(
        functools.partial(merge_kernel, heads),
        in_specs=[scalar, outside] + [whole] * len(flat),
        out_specs=distant,
        out_shape=shape,
        scratch_shapes=[
            pltpu.VMEM(shape.shape, shape.dtype),
            pltpu.SemaphoreType.DMA((heads,)),
        ],
        compiler_params=params(8),
        name="merge",
    )(valid, after, *flat)


def route_blocks(kv_local, state_local, owner_row, index_row):
    parties = lax.axis_size("pool")
    myself = lax.axis_index("pool")
    pages = kv_local.shape[0]
    capacity = max(1, 2 * pages // parties)
    sessions = jnp.arange(parties, dtype=jnp.int32)
    table = (
        (owner_row[:, None] == sessions[None, :]).astype(jnp.int32).reshape(parties, pages, parties)
    )
    before = jnp.cumsum(table, axis=1) - table
    ranks = jnp.sum(before * table, axis=2)
    owners = owner_row.reshape(parties, pages)
    my_owner = lax.dynamic_index_in_dim(owners, myself, 0, keepdims=False)
    device_rank = lax.dynamic_index_in_dim(ranks, myself, 0, keepdims=False)

    def spread(array):
        empty = jnp.zeros((parties, capacity) + array.shape[1:], array.dtype)
        sent = empty.at[my_owner, device_rank].set(array)
        return lax.all_to_all(sent, "pool", split_axis=0, concat_axis=0, tiled=True)

    got_kv, got_state = spread(kv_local), spread(state_local)
    flat_place = (sessions[:, None] * capacity + ranks).reshape(-1)
    target = jnp.where(owner_row == myself, index_row, pages)
    where_from = jnp.zeros((pages,), jnp.int32).at[target].set(flat_place, mode="drop")
    return (
        got_kv.reshape((parties * capacity,) + kv_local.shape[1:])[where_from],
        got_state.reshape((parties * capacity,) + state_local.shape[1:])[where_from],
    )


def local(
    kv_pool,
    state_pool,
    block_owner,
    block_index,
    history_len,
    turn_len,
    mixer_in,
    input_proj,
    output_proj,
    step_size,
    decay_rate,
    bypass_factor,
    queries,
    turn_kv,
):
    parties = lax.axis_size("pool")
    segments = lax.axis_size("ctx")
    kv = kv_pool[0]
    pages = kv.shape[0]
    rows = queries.shape[1]
    heads = kv.shape[-1] // HEAD_DIM
    partner = [(i, i ^ 1) for i in range(segments)]
    opposite = [(i, i ^ 2) for i in range(segments)]

    def to_partner(array):
        return lax.ppermute(array, "ctx", partner)

    def to_opposite(array):
        return lax.ppermute(array, "ctx", opposite)

    if parties == 2:
        swap = [(0, 1), (1, 0)]
        moved, rest = [], kv
        for head in range(heads):
            columns = slice(head * HEAD_DIM, (head + 1) * HEAD_DIM)
            if head == 0:
                cut = (rest[:, 0, :, columns], rest[:, 1, :, columns])
            else:
                cut = (rest[..., columns],)
            cut, rest = lax.optimization_barrier((cut, rest))
            moved.append(tuple(lax.ppermute(piece, "pool", swap) for piece in cut))
        padded = jnp.concatenate([state_pool, state_pool[: pages // 8]], axis=0)
        slab = lax.ppermute(padded, "pool", swap)
        table = (block_owner, block_index)
    else:
        table = (block_owner, jnp.arange(pages, dtype=jnp.int32)[None])
        routed, slab = route_blocks(kv, state_pool, block_owner[0], block_index[0])
        moved = [(routed[..., h * HEAD_DIM : (h + 1) * HEAD_DIM],) for h in range(heads)]
    asks = (queries[0], to_opposite(queries[0]))

    early = [tuple(to_partner(row) for row in table), to_partner(turn_kv[0])]
    if parties == 2:
        early.append(to_partner(kv))
    steps, (table_beside, turn_beside, *kv_beside) = lax.optimization_barrier((step_size[0], early))
    turns = (turn_kv[0], turn_beside)
    tables = table + table_beside
    y, s, run = mixer_from_zero(
        turn_len, mixer_in[0], input_proj[0], output_proj[0], steps, decay_rate, bypass_factor
    )
    parts = []
    after = run
    for head in range(heads):
        came, after = lax.optimization_barrier((moved[head], after))
        own_kv, partner_kv = (came,), (tuple(to_partner(piece) for piece in came),)
        if parties == 2:
            own_kv, partner_kv = ((kv,),) + own_kv, (tuple(kv_beside),) + partner_kv
        ask = functools.partial(
            attend,
            head,
            seen=history_len,
            tables=tables,
            queries=asks,
            own_kv=own_kv,
            partner_kv=partner_kv,
            turns=turns,
        )
        if head + 1 < heads:
            sent, o, after = ask(sides=(1, 0), after=after)
        else:
            (sent,) = ask(sides=(1,), after=after)
            o, after = ask(sides=(0,), after=sent)
        parts.append((o, after, to_opposite(sent)))
    slab, after = lax.optimization_barrier((slab, after))
    slabs = (state_pool, slab) if parties == 2 else (slab,)
    mixed, final, after = add_saved(after, turn_len, table, slabs, y, s, run, output_proj[0])
    attended = merge(after, turn_len, parts, rows)
    return (mixed[None], final[None], attended[None])


def solution(mesh):
    return jax.shard_map(
        local,
        mesh=mesh,
        in_specs=(
            P("ctx", "pool", None, None, "head"),
            P("pool", "ctx", "head"),
            P("ctx", None),
            P("ctx", None),
            P("pool"),
            P("pool"),
            P("pool", "head", "ctx", None),
            P("pool", "head", None, None),
            P("pool", "head", None, None),
            P("pool", "head", None),
            P("head"),
            P("head"),
            P("pool", "ctx", "head"),
            P("pool", None, "ctx", "head"),
        ),
        out_specs=(
            P("pool", "head", "ctx", None),
            P("pool", "head", "ctx", None),
            P("pool", "ctx", "head"),
        ),
        check_vma=False,
    )
```

```python
import functools

import jax
import jax.numpy as jnp
from jax import lax
from jax.experimental import pallas as pl
from jax.experimental.pallas import tpu as pltpu
from jax.sharding import PartitionSpec as P

Q_HEADS = 64
KV_HEADS = 8
HEAD_DIM = 128
PER_GROUP = Q_HEADS // KV_HEADS
BLK = 128
HIDDEN = -1e30
TO_POWER = (HEAD_DIM**-0.5) * 1.4426950408889634
STAT_ROWS = 32
SPARE_ROWS = 48
CHUNK = 768
OWNER = 65536

whole = pl.BlockSpec(memory_space=pltpu.VMEM)
scalar = pl.BlockSpec(memory_space=pltpu.SMEM)
outside = pl.BlockSpec(memory_space=pl.ANY)
distant = pl.BlockSpec(memory_space=pltpu.HBM)


def params(mib):
    return pltpu.CompilerParams(vmem_limit_bytes=mib * 2**20)


def locate(kinds, table_ref, pages):
    if kinds == 1:
        return 0, 0
    myself = lax.axis_index("pool")
    kind = jnp.where(table_ref[0, myself * pages] // OWNER == myself, 0, 1).astype(jnp.int32)
    return kind, jnp.where(kind == 0, myself, 1 - myself) * pages


def as_column(row_ref, start, count):
    row = jnp.broadcast_to(row_ref[...], (count, row_ref.shape[1]))
    across = lax.broadcasted_iota(jnp.int32, row.shape, 1)
    down = lax.broadcasted_iota(jnp.int32, row.shape, 0)
    return jnp.sum(jnp.where(across == down + start, row, 0.0), axis=1, keepdims=True)


def mixer_kernel(valid_ref, x_ref, b_ref, c_ref, dt_ref, rate_ref, gain_ref, y_ref, s_ref, run_ref):
    heads, chans, total = x_ref.shape
    start = pl.program_id(0) * heads
    states = b_ref.shape[1]
    rows = heads * chans
    place = lax.broadcasted_iota(jnp.int32, (heads, total), 1)
    steps = jnp.where(place < valid_ref[0], dt_ref[...], 0.0)
    falls = -as_column(rate_ref, start, heads) * steps
    gains = as_column(gain_ref, start, heads)
    first = lax.broadcasted_iota(jnp.int32, (BLK, BLK), 0)
    second = lax.broadcasted_iota(jnp.int32, (BLK, BLK), 1)
    upper = first <= second
    ones_upper = jnp.where(upper, 1.0, 0.0).astype(jnp.float32)
    turned = b_ref[0].T
    state = jnp.zeros((rows, states), jnp.float32)
    base = jnp.zeros((heads, 1), jnp.float32)
    for blk in range(total // BLK):
        span = slice(blk * BLK, (blk + 1) * BLK)
        run = jnp.dot(
            falls[:, span],
            ones_upper,
            precision=lax.Precision.HIGHEST,
            preferred_element_type=jnp.float32,
        )
        run_col = run.T
        last = run[:, BLK - 1 :]
        pairs = jnp.dot(turned[span], c_ref[0, :, span], preferred_element_type=jnp.float32)
        pairs = jnp.where(upper, pairs, 0.0)
        x_blk = x_ref[:, :, span].astype(jnp.float32)
        stepped = (x_blk * steps[:, None, span]).astype(jnp.bfloat16)
        inside = []
        for head in range(heads):
            gap = jnp.minimum(run[head : head + 1, :] - run_col[:, head : head + 1], 0.0)
            mixing = (jnp.exp(gap) * pairs).astype(jnp.bfloat16)
            inside.append(jnp.dot(stepped[head], mixing, preferred_element_type=jnp.float32))
        result = jnp.stack(inside) + gains[:, :, None] * x_blk
        if blk:
            read = jnp.dot(
                state.astype(jnp.bfloat16), c_ref[0, :, span], preferred_element_type=jnp.float32
            )
            result = result + jnp.exp(run)[:, None, :] * read.reshape(heads, chans, BLK)
        y_ref[:, :, span] = result
        weights = jnp.exp(last - run) * steps[:, span]
        weighted = (x_blk * weights[:, None, :]).astype(jnp.bfloat16).reshape(rows, BLK)
        added = jnp.dot(weighted, turned[span], preferred_element_type=jnp.float32)
        kept = jnp.broadcast_to(jnp.exp(last)[:, :, None], (heads, chans, 1)).reshape(rows, 1)
        state = kept * state + added
        run_ref[:, span] = base + run
        base = base + last
    s_ref[...] = state.reshape(heads, chans, states)


def mixer_from_zero(valid, x, b, c, dt, rates, gains):
    heads, chans, total = x.shape
    groups, states, _ = b.shape
    per = heads // groups
    return pl.pallas_call(
        mixer_kernel,
        grid=(groups,),
        in_specs=[
            scalar,
            pl.BlockSpec((per, chans, total), lambda g: (g, 0, 0)),
            pl.BlockSpec((1, states, total), lambda g: (g, 0, 0)),
            pl.BlockSpec((1, states, total), lambda g: (g, 0, 0)),
            pl.BlockSpec((per, total), lambda g: (g, 0)),
            pl.BlockSpec((1, heads), lambda g: (0, 0)),
            pl.BlockSpec((1, heads), lambda g: (0, 0)),
        ],
        out_specs=[
            pl.BlockSpec((per, chans, total), lambda g: (g, 0, 0)),
            pl.BlockSpec((per, chans, states), lambda g: (g, 0, 0)),
            pl.BlockSpec((per, total), lambda g: (g, 0)),
        ],
        out_shape=[
            jax.ShapeDtypeStruct((heads, chans, total), jnp.float32),
            jax.ShapeDtypeStruct((heads, chans, states), jnp.float32),
            jax.ShapeDtypeStruct((heads, total), jnp.float32),
        ],
        compiler_params=params(16),
        cost_estimate=pl.CostEstimate(flops=1, bytes_accessed=1, transcendentals=0),
        name="mixer_from_zero",
    )(valid, x, b, c, dt, rates[None], gains[None])


def saved_kernel(kinds, valid_ref, chosen_ref, *refs):
    refs = refs[1:]
    slabs = refs[:kinds]
    y_ref, s_ref, run_ref, c_ref, out_ref, final_ref, done_ref, start, mixed, final, sems = refs[
        kinds:
    ]
    done_ref[...] = jnp.zeros(done_ref.shape, jnp.float32)
    heads, chans, total = y_ref.shape
    groups, states, _ = c_ref.shape
    per = heads // groups
    copies = []
    chosen = jnp.max(chosen_ref[0])
    for kind in range(kinds):

        @pl.when(chosen == kind)
        def _():
            start[...] = slabs[kind][:heads]

    live = lax.broadcasted_iota(jnp.int32, (1, 1, total), 2) < valid_ref[0]
    some = per // 2
    for part in range(2 * groups):
        group = part // 2
        mine = slice(part * some, (part + 1) * some)
        saved = start[mine]
        fade = jnp.exp(run_ref[mine, :])
        read = jnp.dot(
            saved.reshape(some * chans, states), c_ref[group], preferred_element_type=jnp.float32
        ).reshape(some, chans, total)
        result = y_ref[mine] + fade[:, None, :] * read
        mixed[mine] = jnp.where(live, result, 0.0).astype(jnp.bfloat16)
        kept = fade[:, None, total - 1 :]
        final[mine] = s_ref[mine] + kept * saved.astype(jnp.float32)
        span = pl.ds(part * some, some)
        for held, target in ((mixed, out_ref), (final, final_ref)):
            copies.append(
                pltpu.make_async_copy(held.at[span], target.at[span], sems.at[len(copies)])
            )
            copies[-1].start()
    for copy in copies:
        copy.wait()


def add_saved(after, valid, chosen, slabs, y, s, run, c):
    heads, chans, total = y.shape
    groups, states, _ = c.shape
    return pl.pallas_call(
        functools.partial(saved_kernel, len(slabs)),
        in_specs=[scalar, whole, outside] + [whole] * (len(slabs) + 4),
        out_specs=[distant, distant, whole],
        out_shape=[
            jax.ShapeDtypeStruct((heads, chans, total), jnp.bfloat16),
            jax.ShapeDtypeStruct((heads, chans, states), jnp.float32),
            jax.ShapeDtypeStruct((8, 128), jnp.float32),
        ],
        scratch_shapes=[
            pltpu.VMEM((heads, chans, states), jnp.bfloat16),
            pltpu.VMEM((heads, chans, total), jnp.bfloat16),
            pltpu.VMEM((heads, chans, states), jnp.float32),
            pltpu.SemaphoreType.DMA((4 * groups,)),
        ],
        compiler_params=params(12),
        cost_estimate=pl.CostEstimate(flops=1, bytes_accessed=1, transcendentals=0),
        name="add_saved",
    )(valid, chosen, after, *slabs, y, s, run, c)


def attend_kernel(counts, head, sides, padding, *refs):
    if head == 0:
        seen_ref, table_refs, refs = refs[0], refs[1:3], refs[3:]
    else:
        hidden_ref, chosen_ref, refs = refs[0], refs[1], refs[2:]
    refs = refs[1:]
    q_refs, turn_refs, refs = refs[: len(sides)], refs[len(sides) : len(sides) + 2], refs[len(sides) + 2 :]
    if padding:
        state_ref, refs = refs[0], refs[1:]
    kinds = len(counts)
    kv_refs = ([], [])
    for side in range(2):
        for count in counts:
            kv_refs[side].append(refs[:count])
            refs = refs[count:]
    out_refs = {}
    for asked in sides:
        out_refs[asked], refs = refs[0], refs[1:]
        if asked == 0:
            l_ref, refs = refs[0], refs[1:]
    if padding:
        padded_ref, refs = refs[0], refs[1:]
        mine = lax.axis_index("pool") * state_ref.shape[0]
        for slot in range(state_ref.shape[0]):
            padded_ref[table_refs[0][0, mine + slot] % OWNER] = state_ref[slot]
        padded_ref[-padding:] = state_ref[:padding]
    if head == 0:
        hidden_ref, chosen_ref, refs = refs[0], refs[1], refs[2:]
    keys, turn_keys, values = refs
    pages, page = keys.shape[0] // 2, keys.shape[1]
    rows = q_refs[0].shape[0]
    history = pages * page
    width = PER_GROUP * HEAD_DIM
    segment = lax.axis_index("ctx")
    numbers = (segment, segment ^ 1)
    columns = slice(head * HEAD_DIM, (head + 1) * HEAD_DIM)
    if head == 0:
        found = [locate(kinds, table_refs[side], pages) for side in range(2)]
        chosen = [kind for kind, _ in found]
        for side in range(2):
            chosen_ref[side] = jnp.full(chosen_ref.shape[1:], chosen[side], jnp.int32)
    else:
        chosen = [jnp.max(chosen_ref[side]) for side in range(2)]

    def take_pages(side, kind):
        sources = kv_refs[side][kind]
        lanes = columns if sources[0].shape[-1] > HEAD_DIM else slice(0, HEAD_DIM)
        target = slice(side * pages, (side + 1) * pages)
        for half, place in enumerate((keys, values)):
            if len(sources) == 1:
                taken = sources[0][:pages, half, :, lanes]
            else:
                taken = sources[half][:pages, :, lanes]
            place[target, :, :HEAD_DIM] = taken

    for side in range(2):
        for kind in range(kinds):

            @pl.when(chosen[side] == kind)
            def _():
                take_pages(side, kind)

    if head == 0:
        in_page = lax.broadcasted_iota(jnp.int32, (page, HEAD_DIM), 0)
        seen = seen_ref[0]
        for side in range(2):
            start = numbers[side] * history
            for number in range(pages):
                left = seen - start - (table_refs[side][0, found[side][1] + number] % OWNER) * page
                hidden_ref[side * pages + number] = jnp.where(in_page < left, 0.0, HIDDEN).astype(
                    jnp.bfloat16
                )
    keys[:, :, HEAD_DIM:] = hidden_ref[...]
    values[:, :, HEAD_DIM:] = jnp.ones(
        (values.shape[0], page, HEAD_DIM), jnp.bfloat16
    )
    first = lax.broadcasted_iota(jnp.int32, (rows, rows), 0)
    second = lax.broadcasted_iota(jnp.int32, (rows, rows), 1)
    eye = jnp.where(first == second, 1.0, 0.0).astype(jnp.bfloat16)
    for i, asked in enumerate(sides):
        asking = segment ^ (2 * asked)
        for side in range(2):
            ahead = first + numbers[side] * rows
            turn_keys[i, pl.ds(side * rows, rows), HEAD_DIM:] = jnp.where(
                ahead <= second + asking * rows, 0.0, HIDDEN
            ).astype(jnp.bfloat16)
    turn_pages = rows // page
    for side in range(2):
        for i in range(len(sides)):
            turn_keys[i, pl.ds(side * rows, rows), pl.ds(0, HEAD_DIM)] = turn_refs[side][0, :, columns]
        values[
            pl.ds(2 * pages + side * turn_pages, turn_pages), :, pl.ds(0, HEAD_DIM)
        ] = turn_refs[side][1, :, columns].reshape(turn_pages, page, HEAD_DIM)
    depth = 2 * HEAD_DIM
    all_keys = 2 * history
    lane = lax.broadcasted_iota(jnp.int32, (rows, HEAD_DIM), 1)
    across = (((1,), (1,)), ((), ()))
    at_once = 2
    for which, asked in enumerate(sides):
        out_ref = out_refs[asked]
        stats = jnp.zeros((rows, HEAD_DIM), jnp.float32)
        for batch in range(PER_GROUP // at_once):
            asks = jnp.concatenate(
                [
                    jnp.concatenate(
                        [
                            q_refs[which][:, pl.ds(head * width + (batch * at_once + i) * HEAD_DIM, HEAD_DIM)],
                            eye,
                        ],
                        axis=1,
                    )
                    for i in range(at_once)
                ],
                axis=0,
            )
            peak = summed = None
            for low in range(0, all_keys, CHUNK):
                high = min(low + CHUNK, all_keys)
                scores = lax.dot_general(
                    asks,
                    keys[...].reshape(all_keys, depth)[low:high],
                    across,
                    preferred_element_type=jnp.float32,
                )
                if high == all_keys:
                    new = lax.dot_general(
                        asks, turn_keys[which], across, preferred_element_type=jnp.float32
                    )
                    scores = jnp.concatenate([scores, new], axis=1)
                    high = high + 2 * rows
                top = jnp.max(scores, axis=1, keepdims=True)
                if peak is not None:
                    top = jnp.maximum(top, peak)
                weights = jnp.exp2((scores - top) * TO_POWER).astype(jnp.bfloat16)
                added = jnp.dot(
                    weights,
                    values[...].reshape(all_keys + 2 * rows, depth)[low:high],
                    preferred_element_type=jnp.float32,
                )
                if peak is not None:
                    added = added + summed * jnp.exp2((peak - top) * TO_POWER)
                peak, summed = top, added
            totals = summed[:, HEAD_DIM:]
            mixed = (summed[:, :HEAD_DIM] / totals).astype(jnp.bfloat16)
            level = peak * TO_POWER + jnp.log2(totals)
            span = pl.ds(batch * at_once * rows, at_once * rows)
            out_ref[span] = mixed
            for i in range(at_once):
                stats = jnp.where(
                    lane == batch * at_once + i, level[i * rows : (i + 1) * rows], stats
                )
        stats = stats.T[:PER_GROUP]
        if asked:
            high = stats.astype(jnp.bfloat16).astype(jnp.float32)
            middle = (stats - high).astype(jnp.bfloat16).astype(jnp.float32)
            low = stats - high - middle
            spare = out_ref.shape[0] - PER_GROUP * rows - STAT_ROWS
            if spare:
                out_ref[pl.ds(PER_GROUP * rows + STAT_ROWS, spare)] = jnp.zeros(
                    (spare, HEAD_DIM), jnp.bfloat16
                )
            out_ref[pl.ds(PER_GROUP * rows, STAT_ROWS)] = jnp.concatenate(
                [high, middle, low, jnp.zeros_like(low)], axis=0
            ).astype(jnp.bfloat16)
        else:
            l_ref[...] = stats


def attend(head, sides, pages, marks, after, queries, own_kv, partner_kv, turns, states=None):
    rows = queries[0].shape[0]
    page = own_kv[0][0].shape[-2]
    counts = tuple(len(choice) for choice in own_kv)
    flat = [array for choice in (*own_kv, *partner_kv) for array in choice]
    all_rows = PER_GROUP * rows
    shapes = []
    for asked in sides:
        extra = STAT_ROWS + (SPARE_ROWS if len(sides) == 2 else 0) if asked else 0
        shapes.append(jax.ShapeDtypeStruct((all_rows + extra, HEAD_DIM), jnp.bfloat16))
        if not asked:
            shapes.append(jax.ShapeDtypeStruct((PER_GROUP, rows), jnp.float32))
    asks = [queries[asked] for asked in sides]
    padding = 0
    if states is not None:
        padding = 2
        flat = [states] + flat
        shapes.append(
            jax.ShapeDtypeStruct((states.shape[0] + padding,) + states.shape[1:], states.dtype)
        )
    if head == 0:
        shapes.append(jax.ShapeDtypeStruct((2 * pages, page, HEAD_DIM), jnp.bfloat16))
        shapes.append(jax.ShapeDtypeStruct((2, 8, 128), jnp.int32))
    return pl.pallas_call(
        functools.partial(attend_kernel, counts, head, sides, padding),
        in_specs=([scalar] * 3 if head == 0 else [whole] * 2) + [outside] + [whole] * (2 + len(sides) + len(flat)),
        out_specs=[whole] * len(shapes),
        out_shape=shapes,
        scratch_shapes=[
            pltpu.VMEM((2 * pages, page, 2 * HEAD_DIM), jnp.bfloat16),
            pltpu.VMEM((len(sides), 2 * rows, 2 * HEAD_DIM), jnp.bfloat16),
            pltpu.VMEM((2 * pages + 2 * rows // page, page, 2 * HEAD_DIM), jnp.bfloat16),
        ],
        compiler_params=params(24),
        cost_estimate=pl.CostEstimate(flops=1, bytes_accessed=1, transcendentals=0),
        name=f"attend_{head}_{len(sides)}_{sides[0]}",
    )(*marks, after, *asks, *turns, *flat)


def merge_kernel(head, valid_ref, after_ref, o_ref, l_ref, got_ref, *refs):
    out_ref, held, sem = refs[-3:]
    rows, width = held.shape
    place = lax.axis_index("ctx") * rows + lax.broadcasted_iota(jnp.int32, (rows, HEAD_DIM), 0)
    live = place < valid_ref[0]
    parts = got_ref[pl.ds(PER_GROUP * rows, STAT_ROWS)].astype(jnp.float32)
    level = parts[:PER_GROUP] + parts[PER_GROUP : 2 * PER_GROUP]
    level = level + parts[2 * PER_GROUP : 3 * PER_GROUP]
    share = 1.0 / (1.0 + jnp.exp2(level - l_ref[...]))
    share = jnp.concatenate([share, jnp.zeros((rows - PER_GROUP, rows), jnp.float32)], axis=0).T
    copies = []
    for member in range(PER_GROUP):
        span = pl.ds(member * rows, rows)
        here = o_ref[span].astype(jnp.float32)
        there = got_ref[span].astype(jnp.float32)
        result = there + share[:, member : member + 1] * (here - there)
        lanes = pl.ds(member * HEAD_DIM, HEAD_DIM)
        held[:, lanes] = jnp.where(live, result, 0.0).astype(jnp.bfloat16)
        if member % 4 == 3:
            first = (member - 3) * HEAD_DIM
            copies.append(
                pltpu.make_async_copy(
                    held.at[:, pl.ds(first, 4 * HEAD_DIM)],
                    out_ref.at[:, pl.ds(head * width + first, 4 * HEAD_DIM)],
                    sem.at[member // 4],
                )
            )
            copies[-1].start()
    for copy in copies:
        copy.wait()


def merge(head, heads, after, valid, part, rows, before=None):
    width = PER_GROUP * HEAD_DIM
    extra = [] if before is None else [before]
    return pl.pallas_call(
        functools.partial(merge_kernel, head),
        in_specs=[scalar, outside] + [whole] * len(part) + [distant] * len(extra),
        out_specs=distant,
        out_shape=jax.ShapeDtypeStruct((rows, heads * width), jnp.bfloat16),
        input_output_aliases={2 + len(part): 0} if extra else {},
        scratch_shapes=[
            pltpu.VMEM((rows, width), jnp.bfloat16),
            pltpu.SemaphoreType.DMA((PER_GROUP // 4,)),
        ],
        compiler_params=params(8),
        name=f"merge_{head}",
    )(valid, after, *part, *extra)


def route_blocks(kv_local, state_local, owner_row, index_row):
    parties = lax.axis_size("pool")
    myself = lax.axis_index("pool")
    pages = kv_local.shape[0]
    capacity = max(1, 2 * pages // parties)
    sessions = jnp.arange(parties, dtype=jnp.int32)
    table = (
        (owner_row[:, None] == sessions[None, :]).astype(jnp.int32).reshape(parties, pages, parties)
    )
    before = jnp.cumsum(table, axis=1) - table
    ranks = jnp.sum(before * table, axis=2)
    owners = owner_row.reshape(parties, pages)
    my_owner = lax.dynamic_index_in_dim(owners, myself, 0, keepdims=False)
    device_rank = lax.dynamic_index_in_dim(ranks, myself, 0, keepdims=False)

    def spread(array):
        empty = jnp.zeros((parties, capacity) + array.shape[1:], array.dtype)
        sent = empty.at[my_owner, device_rank].set(array)
        return lax.all_to_all(sent, "pool", split_axis=0, concat_axis=0, tiled=True)

    got_kv, got_state = spread(kv_local), spread(state_local)
    flat_place = (sessions[:, None] * capacity + ranks).reshape(-1)
    target = jnp.where(owner_row == myself, index_row, pages)
    where_from = jnp.zeros((pages,), jnp.int32).at[target].set(flat_place, mode="drop")
    return (
        got_kv.reshape((parties * capacity,) + kv_local.shape[1:])[where_from],
        got_state.reshape((parties * capacity,) + state_local.shape[1:])[where_from],
    )


def local(
    kv_pool,
    state_pool,
    block_owner,
    block_index,
    history_len,
    turn_len,
    mixer_in,
    input_proj,
    output_proj,
    step_size,
    decay_rate,
    bypass_factor,
    queries,
    turn_kv,
):
    parties = lax.axis_size("pool")
    segments = lax.axis_size("ctx")
    kv = kv_pool[0]
    pages = kv.shape[0]
    rows = queries.shape[1]
    heads = kv.shape[-1] // HEAD_DIM
    partner = [(i, i ^ 1) for i in range(segments)]
    opposite = [(i, i ^ 2) for i in range(segments)]

    def to_partner(array):
        return lax.ppermute(array, "ctx", partner)

    def to_opposite(array):
        return lax.ppermute(array, "ctx", opposite)

    if parties == 2:
        swap = [(0, 1), (1, 0)]
        moved, pieces, rest = [], [], kv
        for head in range(heads):
            columns = slice(head * HEAD_DIM, (head + 1) * HEAD_DIM)
            cut = rest[..., columns]
            if head:
                cut = jnp.concatenate([cut, cut[:1]], axis=0)
            cut = (cut,)
            cut, rest = lax.optimization_barrier((cut, rest))
            pieces.append(cut)
            moved.append(tuple(lax.ppermute(piece, "pool", swap) for piece in cut))
        table = block_owner * OWNER + block_index
    else:
        table = jnp.arange(pages, dtype=jnp.int32)[None]
        routed, slab = route_blocks(kv, state_pool, block_owner[0], block_index[0])
        moved = [(routed[..., h * HEAD_DIM : (h + 1) * HEAD_DIM],) for h in range(heads)]
    asks = (queries[0], to_opposite(queries[0]))

    turns = (turn_kv[0], to_partner(turn_kv[0]))
    tables = (table, to_partner(table))
    y, s, run = mixer_from_zero(
        turn_len, mixer_in[0], input_proj[0], output_proj[0], step_size[0], decay_rate, bypass_factor
    )
    parts = []
    after = run
    marks = (history_len, *tables)
    for head in range(heads):
        came, after = lax.optimization_barrier((moved[head], after))
        own_kv, partner_kv = (came,), (tuple(to_partner(piece) for piece in came),)
        if parties == 2:
            beside = tuple(to_partner(piece) for piece in pieces[head])
            own_kv, partner_kv = (pieces[head],) + own_kv, (beside,) + partner_kv
        ask = functools.partial(
            attend,
            head,
            pages=pages,
            marks=marks,
            queries=asks,
            own_kv=own_kv,
            partner_kv=partner_kv,
            turns=turns,
        )
        if head + 1 < heads:
            states = state_pool if parties == 2 and head == 0 else None
            sent, o, after, *padded, hidden, chosen = ask(sides=(1, 0), after=after, states=states)
            marks = (hidden, chosen)
            if padded:
                ordered = padded[0]
                slab = lax.ppermute(ordered, "pool", swap)
        else:
            (sent,) = ask(sides=(1,), after=after)
            o, after = ask(sides=(0,), after=sent)
        parts.append((o, after, to_opposite(sent)))
    slab, after = lax.optimization_barrier((slab, after))
    slabs = (ordered, slab) if parties == 2 else (slab,)
    mixed, final, after = add_saved(after, turn_len, chosen, slabs, y, s, run, output_proj[0])
    attended = None
    for head in range(heads):
        attended = merge(head, heads, after, turn_len, parts[head], rows, attended)
    return (mixed[None], final[None], attended[None])


def solution(mesh):
    return jax.shard_map(
        local,
        mesh=mesh,
        in_specs=(
            P("ctx", "pool", None, None, "head"),
            P("pool", "ctx", "head"),
            P("ctx", None),
            P("ctx", None),
            P("pool"),
            P("pool"),
            P("pool", "head", "ctx", None),
            P("pool", "head", None, None),
            P("pool", "head", None, None),
            P("pool", "head", None),
            P("head"),
            P("head"),
            P("pool", "ctx", "head"),
            P("pool", None, "ctx", "head"),
        ),
        out_specs=(
            P("pool", "head", "ctx", None),
            P("pool", "head", "ctx", None),
            P("pool", "ctx", "head"),
        ),
        check_vma=False,
    )
```

```python
import functools

import jax
import jax.numpy as jnp
from jax import lax
from jax.experimental import pallas as pl
from jax.experimental.pallas import tpu as pltpu
from jax.sharding import PartitionSpec as P

Q_HEADS = 64
KV_HEADS = 8
HEAD_DIM = 128
PER_GROUP = Q_HEADS // KV_HEADS
BLK = 128
HIDDEN = -1e30
TO_POWER = (HEAD_DIM**-0.5) * 1.4426950408889634
STAT_ROWS = 32
SPARE_ROWS = 48
CHUNK = 768
OWNER = 65536

whole = pl.BlockSpec(memory_space=pltpu.VMEM)
scalar = pl.BlockSpec(memory_space=pltpu.SMEM)
outside = pl.BlockSpec(memory_space=pl.ANY)
distant = pl.BlockSpec(memory_space=pltpu.HBM)


def params(mib):
    return pltpu.CompilerParams(vmem_limit_bytes=mib * 2**20)


def locate(kinds, table_ref, pages):
    if kinds == 1:
        return 0, 0
    myself = lax.axis_index("pool")
    kind = jnp.where(table_ref[0, myself * pages] // OWNER == myself, 0, 1).astype(jnp.int32)
    return kind, jnp.where(kind == 0, myself, 1 - myself) * pages


def as_column(row_ref, start, count):
    row = jnp.broadcast_to(row_ref[...], (count, row_ref.shape[1]))
    across = lax.broadcasted_iota(jnp.int32, row.shape, 1)
    down = lax.broadcasted_iota(jnp.int32, row.shape, 0)
    return jnp.sum(jnp.where(across == down + start, row, 0.0), axis=1, keepdims=True)


def mixer_kernel(valid_ref, x_ref, b_ref, c_ref, dt_ref, rate_ref, gain_ref, y_ref, s_ref, run_ref):
    heads, chans, total = x_ref.shape
    start = pl.program_id(0) * heads
    states = b_ref.shape[1]
    rows = heads * chans
    place = lax.broadcasted_iota(jnp.int32, (heads, total), 1)
    steps = jnp.where(place < valid_ref[0], dt_ref[...], 0.0)
    falls = -as_column(rate_ref, start, heads) * steps
    gains = as_column(gain_ref, start, heads)
    first = lax.broadcasted_iota(jnp.int32, (BLK, BLK), 0)
    second = lax.broadcasted_iota(jnp.int32, (BLK, BLK), 1)
    upper = first <= second
    ones_upper = jnp.where(upper, 1.0, 0.0).astype(jnp.float32)
    turned = b_ref[0].T
    state = jnp.zeros((rows, states), jnp.float32)
    base = jnp.zeros((heads, 1), jnp.float32)
    for blk in range(total // BLK):
        span = slice(blk * BLK, (blk + 1) * BLK)
        run = jnp.dot(
            falls[:, span],
            ones_upper,
            precision=lax.Precision.HIGHEST,
            preferred_element_type=jnp.float32,
        )
        run_col = run.T
        last = run[:, BLK - 1 :]
        pairs = jnp.dot(turned[span], c_ref[0, :, span], preferred_element_type=jnp.float32)
        pairs = jnp.where(upper, pairs, 0.0)
        x_blk = x_ref[:, :, span].astype(jnp.float32)
        stepped = (x_blk * steps[:, None, span]).astype(jnp.bfloat16)
        inside = []
        for head in range(heads):
            gap = jnp.minimum(run[head : head + 1, :] - run_col[:, head : head + 1], 0.0)
            mixing = (jnp.exp(gap) * pairs).astype(jnp.bfloat16)
            inside.append(jnp.dot(stepped[head], mixing, preferred_element_type=jnp.float32))
        result = jnp.stack(inside) + gains[:, :, None] * x_blk
        if blk:
            read = jnp.dot(
                state.astype(jnp.bfloat16), c_ref[0, :, span], preferred_element_type=jnp.float32
            )
            result = result + jnp.exp(run)[:, None, :] * read.reshape(heads, chans, BLK)
        y_ref[:, :, span] = result
        weights = jnp.exp(last - run) * steps[:, span]
        weighted = (x_blk * weights[:, None, :]).astype(jnp.bfloat16).reshape(rows, BLK)
        added = jnp.dot(weighted, turned[span], preferred_element_type=jnp.float32)
        kept = jnp.broadcast_to(jnp.exp(last)[:, :, None], (heads, chans, 1)).reshape(rows, 1)
        state = kept * state + added
        run_ref[:, span] = base + run
        base = base + last
    s_ref[...] = state.reshape(heads, chans, states)


def mixer_from_zero(valid, x, b, c, dt, rates, gains):
    heads, chans, total = x.shape
    groups, states, _ = b.shape
    per = heads // groups
    return pl.pallas_call(
        mixer_kernel,
        grid=(groups,),
        in_specs=[
            scalar,
            pl.BlockSpec((per, chans, total), lambda g: (g, 0, 0)),
            pl.BlockSpec((1, states, total), lambda g: (g, 0, 0)),
            pl.BlockSpec((1, states, total), lambda g: (g, 0, 0)),
            pl.BlockSpec((per, total), lambda g: (g, 0)),
            pl.BlockSpec((1, heads), lambda g: (0, 0)),
            pl.BlockSpec((1, heads), lambda g: (0, 0)),
        ],
        out_specs=[
            pl.BlockSpec((per, chans, total), lambda g: (g, 0, 0)),
            pl.BlockSpec((per, chans, states), lambda g: (g, 0, 0)),
            pl.BlockSpec((per, total), lambda g: (g, 0)),
        ],
        out_shape=[
            jax.ShapeDtypeStruct((heads, chans, total), jnp.float32),
            jax.ShapeDtypeStruct((heads, chans, states), jnp.float32),
            jax.ShapeDtypeStruct((heads, total), jnp.float32),
        ],
        compiler_params=params(16),
        cost_estimate=pl.CostEstimate(flops=1, bytes_accessed=1, transcendentals=0),
        name="mixer_from_zero",
    )(valid, x, b, c, dt, rates[None], gains[None])


def saved_kernel(kinds, valid_ref, chosen_ref, *refs):
    refs = refs[1:]
    slabs = refs[:kinds]
    y_ref, s_ref, run_ref, c_ref, out_ref, final_ref, done_ref, start, mixed, final, sems = refs[
        kinds:
    ]
    done_ref[...] = jnp.zeros(done_ref.shape, jnp.float32)
    heads, chans, total = y_ref.shape
    groups, states, _ = c_ref.shape
    per = heads // groups
    copies = []
    chosen = jnp.max(chosen_ref[0])
    for kind in range(kinds):

        @pl.when(chosen == kind)
        def _():
            start[...] = slabs[kind][:heads]

    live = lax.broadcasted_iota(jnp.int32, (1, 1, total), 2) < valid_ref[0]
    some = per // 2
    for part in range(2 * groups):
        group = part // 2
        mine = slice(part * some, (part + 1) * some)
        saved = start[mine]
        fade = jnp.exp(run_ref[mine, :])
        read = jnp.dot(
            saved.reshape(some * chans, states), c_ref[group], preferred_element_type=jnp.float32
        ).reshape(some, chans, total)
        result = y_ref[mine] + fade[:, None, :] * read
        mixed[mine] = jnp.where(live, result, 0.0).astype(jnp.bfloat16)
        kept = fade[:, None, total - 1 :]
        final[mine] = s_ref[mine] + kept * saved.astype(jnp.float32)
        span = pl.ds(part * some, some)
        for held, target in ((mixed, out_ref), (final, final_ref)):
            copies.append(
                pltpu.make_async_copy(held.at[span], target.at[span], sems.at[len(copies)])
            )
            copies[-1].start()
    for copy in copies:
        copy.wait()


def add_saved(after, valid, chosen, slabs, y, s, run, c):
    heads, chans, total = y.shape
    groups, states, _ = c.shape
    return pl.pallas_call(
        functools.partial(saved_kernel, len(slabs)),
        in_specs=[scalar, whole, outside] + [whole] * (len(slabs) + 4),
        out_specs=[distant, distant, whole],
        out_shape=[
            jax.ShapeDtypeStruct((heads, chans, total), jnp.bfloat16),
            jax.ShapeDtypeStruct((heads, chans, states), jnp.float32),
            jax.ShapeDtypeStruct((8, 128), jnp.float32),
        ],
        scratch_shapes=[
            pltpu.VMEM((heads, chans, states), jnp.bfloat16),
            pltpu.VMEM((heads, chans, total), jnp.bfloat16),
            pltpu.VMEM((heads, chans, states), jnp.float32),
            pltpu.SemaphoreType.DMA((4 * groups,)),
        ],
        compiler_params=params(12),
        cost_estimate=pl.CostEstimate(flops=1, bytes_accessed=1, transcendentals=0),
        name="add_saved",
    )(valid, chosen, after, *slabs, y, s, run, c)


def attend_kernel(counts, head, sides, padding, *refs):
    if head == 0:
        seen_ref, table_refs, refs = refs[0], refs[1:3], refs[3:]
    else:
        hidden_ref, chosen_ref, refs = refs[0], refs[1], refs[2:]
    refs = refs[1:]
    q_refs, turn_refs, refs = refs[: len(sides)], refs[len(sides) : len(sides) + 2], refs[len(sides) + 2 :]
    if padding:
        state_ref, refs = refs[0], refs[1:]
    kinds = len(counts)
    kv_refs = ([], [])
    for side in range(2):
        for count in counts:
            kv_refs[side].append(refs[:count])
            refs = refs[count:]
    out_refs = {}
    for asked in sides:
        out_refs[asked], refs = refs[0], refs[1:]
        if asked == 0:
            l_ref, refs = refs[0], refs[1:]
    if padding:
        padded_ref, refs = refs[0], refs[1:]
        mine = lax.axis_index("pool") * state_ref.shape[0]
        for slot in range(state_ref.shape[0]):
            padded_ref[table_refs[0][0, mine + slot] % OWNER] = state_ref[slot]
        padded_ref[-padding:] = state_ref[:padding]
    if head == 0:
        hidden_ref, chosen_ref, refs = refs[0], refs[1], refs[2:]
    keys, turn_keys, values = refs
    pages, page = keys.shape[0] // 2, keys.shape[1]
    rows = q_refs[0].shape[0]
    history = pages * page
    width = PER_GROUP * HEAD_DIM
    segment = lax.axis_index("ctx")
    numbers = (segment, segment ^ 1)
    columns = slice(head * HEAD_DIM, (head + 1) * HEAD_DIM)
    if head == 0:
        found = [locate(kinds, table_refs[side], pages) for side in range(2)]
        chosen = [kind for kind, _ in found]
        for side in range(2):
            chosen_ref[side] = jnp.full(chosen_ref.shape[1:], chosen[side], jnp.int32)
    else:
        chosen = [jnp.max(chosen_ref[side]) for side in range(2)]

    def take_pages(side, kind):
        sources = kv_refs[side][kind]
        lanes = columns if sources[0].shape[-1] > HEAD_DIM else slice(0, HEAD_DIM)
        target = slice(side * pages, (side + 1) * pages)
        for half, place in enumerate((keys, values)):
            if len(sources) == 1:
                taken = sources[0][:pages, half, :, lanes]
            else:
                taken = sources[half][:pages, :, lanes]
            place[target, :, :HEAD_DIM] = taken

    for side in range(2):
        for kind in range(kinds):

            @pl.when(chosen[side] == kind)
            def _():
                take_pages(side, kind)

    if head == 0:
        in_page = lax.broadcasted_iota(jnp.int32, (page, HEAD_DIM), 0)
        seen = seen_ref[0]
        for side in range(2):
            start = numbers[side] * history
            for number in range(pages):
                left = seen - start - (table_refs[side][0, found[side][1] + number] % OWNER) * page
                hidden_ref[side * pages + number] = jnp.where(in_page < left, 0.0, HIDDEN).astype(
                    jnp.bfloat16
                )
    keys[:, :, HEAD_DIM:] = hidden_ref[...]
    values[:, :, HEAD_DIM:] = jnp.ones(
        (values.shape[0], page, HEAD_DIM), jnp.bfloat16
    )
    first = lax.broadcasted_iota(jnp.int32, (rows, rows), 0)
    second = lax.broadcasted_iota(jnp.int32, (rows, rows), 1)
    eye = jnp.where(first == second, 1.0, 0.0).astype(jnp.bfloat16)
    for i, asked in enumerate(sides):
        asking = segment ^ (2 * asked)
        for side in range(2):
            ahead = first + numbers[side] * rows
            turn_keys[i, pl.ds(side * rows, rows), HEAD_DIM:] = jnp.where(
                ahead <= second + asking * rows, 0.0, HIDDEN
            ).astype(jnp.bfloat16)
    turn_pages = rows // page
    for side in range(2):
        for i in range(len(sides)):
            turn_keys[i, pl.ds(side * rows, rows), pl.ds(0, HEAD_DIM)] = turn_refs[side][0, :, columns]
        values[
            pl.ds(2 * pages + side * turn_pages, turn_pages), :, pl.ds(0, HEAD_DIM)
        ] = turn_refs[side][1, :, columns].reshape(turn_pages, page, HEAD_DIM)
    depth = 2 * HEAD_DIM
    all_keys = 2 * history
    lane = lax.broadcasted_iota(jnp.int32, (rows, HEAD_DIM), 1)
    across = (((1,), (1,)), ((), ()))
    at_once = 2
    for which, asked in enumerate(sides):
        out_ref = out_refs[asked]
        stats = jnp.zeros((rows, HEAD_DIM), jnp.float32)
        for batch in range(PER_GROUP // at_once):
            asks = jnp.concatenate(
                [
                    jnp.concatenate(
                        [
                            q_refs[which][:, pl.ds(head * width + (batch * at_once + i) * HEAD_DIM, HEAD_DIM)],
                            eye,
                        ],
                        axis=1,
                    )
                    for i in range(at_once)
                ],
                axis=0,
            )
            peak = summed = None
            for low in range(0, all_keys, CHUNK):
                high = min(low + CHUNK, all_keys)
                scores = lax.dot_general(
                    asks,
                    keys[...].reshape(all_keys, depth)[low:high],
                    across,
                    preferred_element_type=jnp.float32,
                )
                if high == all_keys:
                    new = lax.dot_general(
                        asks, turn_keys[which], across, preferred_element_type=jnp.float32
                    )
                    scores = jnp.concatenate([scores, new], axis=1)
                    high = high + 2 * rows
                top = jnp.max(scores, axis=1, keepdims=True)
                if peak is not None:
                    top = jnp.maximum(top, peak)
                weights = jnp.exp2((scores - top) * TO_POWER).astype(jnp.bfloat16)
                added = jnp.dot(
                    weights,
                    values[...].reshape(all_keys + 2 * rows, depth)[low:high],
                    preferred_element_type=jnp.float32,
                )
                if peak is not None:
                    added = added + summed * jnp.exp2((peak - top) * TO_POWER)
                peak, summed = top, added
            totals = summed[:, HEAD_DIM:]
            mixed = (summed[:, :HEAD_DIM] / totals).astype(jnp.bfloat16)
            level = peak * TO_POWER + jnp.log2(totals)
            span = pl.ds(batch * at_once * rows, at_once * rows)
            out_ref[span] = mixed
            for i in range(at_once):
                stats = jnp.where(
                    lane == batch * at_once + i, level[i * rows : (i + 1) * rows], stats
                )
        stats = stats.T[:PER_GROUP]
        if asked:
            high = stats.astype(jnp.bfloat16).astype(jnp.float32)
            middle = (stats - high).astype(jnp.bfloat16).astype(jnp.float32)
            low = stats - high - middle
            spare = out_ref.shape[0] - PER_GROUP * rows - STAT_ROWS
            if spare:
                out_ref[pl.ds(PER_GROUP * rows + STAT_ROWS, spare)] = jnp.zeros(
                    (spare, HEAD_DIM), jnp.bfloat16
                )
            out_ref[pl.ds(PER_GROUP * rows, STAT_ROWS)] = jnp.concatenate(
                [high, middle, low, jnp.zeros_like(low)], axis=0
            ).astype(jnp.bfloat16)
        else:
            l_ref[...] = stats


def attend(head, sides, pages, marks, after, queries, own_kv, partner_kv, turns, states=None):
    rows = queries[0].shape[0]
    page = own_kv[0][0].shape[-2]
    counts = tuple(len(choice) for choice in own_kv)
    flat = [array for choice in (*own_kv, *partner_kv) for array in choice]
    all_rows = PER_GROUP * rows
    shapes = []
    for asked in sides:
        extra = STAT_ROWS + (SPARE_ROWS if len(sides) == 2 else 0) if asked else 0
        shapes.append(jax.ShapeDtypeStruct((all_rows + extra, HEAD_DIM), jnp.bfloat16))
        if not asked:
            shapes.append(jax.ShapeDtypeStruct((PER_GROUP, rows), jnp.float32))
    asks = [queries[asked] for asked in sides]
    padding = 0
    if states is not None:
        padding = 2
        flat = [states] + flat
        shapes.append(
            jax.ShapeDtypeStruct((states.shape[0] + padding,) + states.shape[1:], states.dtype)
        )
    if head == 0:
        shapes.append(jax.ShapeDtypeStruct((2 * pages, page, HEAD_DIM), jnp.bfloat16))
        shapes.append(jax.ShapeDtypeStruct((2, 8, 128), jnp.int32))
    return pl.pallas_call(
        functools.partial(attend_kernel, counts, head, sides, padding),
        in_specs=([scalar] * 3 if head == 0 else [whole] * 2) + [outside] + [whole] * (2 + len(sides) + len(flat)),
        out_specs=[whole] * len(shapes),
        out_shape=shapes,
        scratch_shapes=[
            pltpu.VMEM((2 * pages, page, 2 * HEAD_DIM), jnp.bfloat16),
            pltpu.VMEM((len(sides), 2 * rows, 2 * HEAD_DIM), jnp.bfloat16),
            pltpu.VMEM((2 * pages + 2 * rows // page, page, 2 * HEAD_DIM), jnp.bfloat16),
        ],
        compiler_params=params(24),
        cost_estimate=pl.CostEstimate(flops=1, bytes_accessed=1, transcendentals=0),
        name=f"attend_{head}_{len(sides)}_{sides[0]}",
    )(*marks, after, *asks, *turns, *flat)


def merge_kernel(head, valid_ref, after_ref, o_ref, l_ref, got_ref, *refs):
    out_ref, held, sem = refs[-3:]
    rows, width = held.shape
    place = lax.axis_index("ctx") * rows + lax.broadcasted_iota(jnp.int32, (rows, HEAD_DIM), 0)
    live = place < valid_ref[0]
    parts = got_ref[pl.ds(PER_GROUP * rows, STAT_ROWS)].astype(jnp.float32)
    level = parts[:PER_GROUP] + parts[PER_GROUP : 2 * PER_GROUP]
    level = level + parts[2 * PER_GROUP : 3 * PER_GROUP]
    share = 1.0 / (1.0 + jnp.exp2(level - l_ref[...]))
    share = jnp.concatenate([share, jnp.zeros((rows - PER_GROUP, rows), jnp.float32)], axis=0).T
    copies = []
    for member in range(PER_GROUP):
        span = pl.ds(member * rows, rows)
        here = o_ref[span].astype(jnp.float32)
        there = got_ref[span].astype(jnp.float32)
        result = there + share[:, member : member + 1] * (here - there)
        lanes = pl.ds(member * HEAD_DIM, HEAD_DIM)
        held[:, lanes] = jnp.where(live, result, 0.0).astype(jnp.bfloat16)
        if member % 4 == 3:
            first = (member - 3) * HEAD_DIM
            copies.append(
                pltpu.make_async_copy(
                    held.at[:, pl.ds(first, 4 * HEAD_DIM)],
                    out_ref.at[:, pl.ds(head * width + first, 4 * HEAD_DIM)],
                    sem.at[member // 4],
                )
            )
            copies[-1].start()
    for copy in copies:
        copy.wait()


def merge(head, heads, after, valid, part, rows, before=None):
    width = PER_GROUP * HEAD_DIM
    extra = [] if before is None else [before]
    return pl.pallas_call(
        functools.partial(merge_kernel, head),
        in_specs=[scalar, outside] + [whole] * len(part) + [distant] * len(extra),
        out_specs=distant,
        out_shape=jax.ShapeDtypeStruct((rows, heads * width), jnp.bfloat16),
        input_output_aliases={2 + len(part): 0} if extra else {},
        scratch_shapes=[
            pltpu.VMEM((rows, width), jnp.bfloat16),
            pltpu.SemaphoreType.DMA((PER_GROUP // 4,)),
        ],
        compiler_params=params(8),
        name=f"merge_{head}",
    )(valid, after, *part, *extra)


def route_blocks(kv_local, state_local, owner_row, index_row):
    parties = lax.axis_size("pool")
    myself = lax.axis_index("pool")
    pages = kv_local.shape[0]
    capacity = max(1, 2 * pages // parties)
    sessions = jnp.arange(parties, dtype=jnp.int32)
    table = (
        (owner_row[:, None] == sessions[None, :]).astype(jnp.int32).reshape(parties, pages, parties)
    )
    before = jnp.cumsum(table, axis=1) - table
    ranks = jnp.sum(before * table, axis=2)
    owners = owner_row.reshape(parties, pages)
    my_owner = lax.dynamic_index_in_dim(owners, myself, 0, keepdims=False)
    device_rank = lax.dynamic_index_in_dim(ranks, myself, 0, keepdims=False)

    def spread(array):
        empty = jnp.zeros((parties, capacity) + array.shape[1:], array.dtype)
        sent = empty.at[my_owner, device_rank].set(array)
        return lax.all_to_all(sent, "pool", split_axis=0, concat_axis=0, tiled=True)

    got_kv, got_state = spread(kv_local), spread(state_local)
    flat_place = (sessions[:, None] * capacity + ranks).reshape(-1)
    target = jnp.where(owner_row == myself, index_row, pages)
    where_from = jnp.zeros((pages,), jnp.int32).at[target].set(flat_place, mode="drop")
    return (
        got_kv.reshape((parties * capacity,) + kv_local.shape[1:])[where_from],
        got_state.reshape((parties * capacity,) + state_local.shape[1:])[where_from],
    )


def local(
    kv_pool,
    state_pool,
    block_owner,
    block_index,
    history_len,
    turn_len,
    mixer_in,
    input_proj,
    output_proj,
    step_size,
    decay_rate,
    bypass_factor,
    queries,
    turn_kv,
):
    parties = lax.axis_size("pool")
    segments = lax.axis_size("ctx")
    kv = kv_pool[0]
    pages = kv.shape[0]
    rows = queries.shape[1]
    heads = kv.shape[-1] // HEAD_DIM
    partner = [(i, i ^ 1) for i in range(segments)]
    opposite = [(i, i ^ 2) for i in range(segments)]

    def to_partner(array):
        return lax.ppermute(array, "ctx", partner)

    def to_opposite(array):
        return lax.ppermute(array, "ctx", opposite)

    if parties == 2:
        swap = [(0, 1), (1, 0)]
        moved, pieces, rest = [], [], kv
        for head in range(heads):
            columns = slice(head * HEAD_DIM, (head + 1) * HEAD_DIM)
            cut = rest[..., columns]
            if head:
                cut = jnp.concatenate([cut, cut[:1]], axis=0)
            cut = (cut,)
            cut, rest = lax.optimization_barrier((cut, rest))
            pieces.append(cut)
            moved.append(tuple(lax.ppermute(piece, "pool", swap) for piece in cut))
        table = block_owner * OWNER + block_index
    else:
        table = jnp.arange(pages, dtype=jnp.int32)[None]
        routed, slab = route_blocks(kv, state_pool, block_owner[0], block_index[0])
        moved = [(routed[..., h * HEAD_DIM : (h + 1) * HEAD_DIM],) for h in range(heads)]
    asks = (queries[0], to_opposite(queries[0]))

    turns = (turn_kv[0], to_partner(turn_kv[0]))
    steps, table_beside = lax.optimization_barrier((step_size[0], to_partner(table)))
    tables = (table, table_beside)
    y, s, run = mixer_from_zero(
        turn_len, mixer_in[0], input_proj[0], output_proj[0], steps, decay_rate, bypass_factor
    )
    parts = []
    after = run
    marks = (history_len, *tables)
    for head in range(heads):
        came, after = lax.optimization_barrier((moved[head], after))
        own_kv, partner_kv = (came,), (tuple(to_partner(piece) for piece in came),)
        if parties == 2:
            beside = tuple(to_partner(piece) for piece in pieces[head])
            own_kv, partner_kv = (pieces[head],) + own_kv, (beside,) + partner_kv
        ask = functools.partial(
            attend,
            head,
            pages=pages,
            marks=marks,
            queries=asks,
            own_kv=own_kv,
            partner_kv=partner_kv,
            turns=turns,
        )
        if head + 1 < heads:
            states = state_pool if parties == 2 and head == 0 else None
            sent, o, after, *padded, hidden, chosen = ask(sides=(1, 0), after=after, states=states)
            marks = (hidden, chosen)
            if padded:
                ordered = padded[0]
                slab = lax.ppermute(ordered, "pool", swap)
        else:
            (sent,) = ask(sides=(1,), after=after)
            o, after = ask(sides=(0,), after=sent)
        parts.append((o, after, to_opposite(sent)))
    slab, after = lax.optimization_barrier((slab, after))
    slabs = (ordered, slab) if parties == 2 else (slab,)
    mixed, final, after = add_saved(after, turn_len, chosen, slabs, y, s, run, output_proj[0])
    attended = None
    for head in range(heads):
        attended = merge(head, heads, after, turn_len, parts[head], rows, attended)
    return (mixed[None], final[None], attended[None])


def solution(mesh):
    return jax.shard_map(
        local,
        mesh=mesh,
        in_specs=(
            P("ctx", "pool", None, None, "head"),
            P("pool", "ctx", "head"),
            P("ctx", None),
            P("ctx", None),
            P("pool"),
            P("pool"),
            P("pool", "head", "ctx", None),
            P("pool", "head", None, None),
            P("pool", "head", None, None),
            P("pool", "head", None),
            P("head"),
            P("head"),
            P("pool", "ctx", "head"),
            P("pool", None, "ctx", "head"),
        ),
        out_specs=(
            P("pool", "head", "ctx", None),
            P("pool", "head", "ctx", None),
            P("pool", "ctx", "head"),
        ),
        check_vma=False,
    )
```

```python
import functools

import jax
import jax.numpy as jnp
from jax import lax
from jax.experimental import pallas as pl
from jax.experimental.pallas import tpu as pltpu
from jax.sharding import PartitionSpec as P

Q_HEADS = 64
KV_HEADS = 8
HEAD_DIM = 128
PER_GROUP = Q_HEADS // KV_HEADS
BLK = 128
HIDDEN = -1e30
TO_POWER = (HEAD_DIM**-0.5) * 1.4426950408889634
STAT_ROWS = 32
SPARE_ROWS = 48
CHUNK = 768
OWNER = 65536

whole = pl.BlockSpec(memory_space=pltpu.VMEM)
scalar = pl.BlockSpec(memory_space=pltpu.SMEM)
outside = pl.BlockSpec(memory_space=pl.ANY)
distant = pl.BlockSpec(memory_space=pltpu.HBM)


def params(mib):
    return pltpu.CompilerParams(vmem_limit_bytes=mib * 2**20)


def locate(kinds, table_ref, pages):
    if kinds == 1:
        return 0, 0
    myself = lax.axis_index("pool")
    kind = jnp.where(table_ref[0, myself * pages] // OWNER == myself, 0, 1).astype(jnp.int32)
    return kind, jnp.where(kind == 0, myself, 1 - myself) * pages


def as_column(row_ref, start, count):
    row = jnp.broadcast_to(row_ref[...], (count, row_ref.shape[1]))
    across = lax.broadcasted_iota(jnp.int32, row.shape, 1)
    down = lax.broadcasted_iota(jnp.int32, row.shape, 0)
    return jnp.sum(jnp.where(across == down + start, row, 0.0), axis=1, keepdims=True)


def mixer_kernel(valid_ref, x_ref, b_ref, c_ref, dt_ref, rate_ref, gain_ref, y_ref, s_ref, run_ref):
    heads, chans, total = x_ref.shape
    start = pl.program_id(0) * heads
    states = b_ref.shape[1]
    rows = heads * chans
    place = lax.broadcasted_iota(jnp.int32, (heads, total), 1)
    steps = jnp.where(place < valid_ref[0], dt_ref[...], 0.0)
    falls = -as_column(rate_ref, start, heads) * steps
    gains = as_column(gain_ref, start, heads)
    first = lax.broadcasted_iota(jnp.int32, (BLK, BLK), 0)
    second = lax.broadcasted_iota(jnp.int32, (BLK, BLK), 1)
    upper = first <= second
    ones_upper = jnp.where(upper, 1.0, 0.0).astype(jnp.float32)
    turned = b_ref[0].T
    state = jnp.zeros((rows, states), jnp.float32)
    base = jnp.zeros((heads, 1), jnp.float32)
    for blk in range(total // BLK):
        span = slice(blk * BLK, (blk + 1) * BLK)
        run = jnp.dot(
            falls[:, span],
            ones_upper,
            precision=lax.Precision.HIGHEST,
            preferred_element_type=jnp.float32,
        )
        run_col = run.T
        last = run[:, BLK - 1 :]
        pairs = jnp.dot(turned[span], c_ref[0, :, span], preferred_element_type=jnp.float32)
        pairs = jnp.where(upper, pairs, 0.0)
        x_blk = x_ref[:, :, span].astype(jnp.float32)
        stepped = (x_blk * steps[:, None, span]).astype(jnp.bfloat16)
        inside = []
        for head in range(heads):
            gap = jnp.minimum(run[head : head + 1, :] - run_col[:, head : head + 1], 0.0)
            mixing = (jnp.exp(gap) * pairs).astype(jnp.bfloat16)
            inside.append(jnp.dot(stepped[head], mixing, preferred_element_type=jnp.float32))
        result = jnp.stack(inside) + gains[:, :, None] * x_blk
        if blk:
            read = jnp.dot(
                state.astype(jnp.bfloat16), c_ref[0, :, span], preferred_element_type=jnp.float32
            )
            result = result + jnp.exp(run)[:, None, :] * read.reshape(heads, chans, BLK)
        y_ref[:, :, span] = result
        weights = jnp.exp(last - run) * steps[:, span]
        weighted = (x_blk * weights[:, None, :]).astype(jnp.bfloat16).reshape(rows, BLK)
        added = jnp.dot(weighted, turned[span], preferred_element_type=jnp.float32)
        kept = jnp.broadcast_to(jnp.exp(last)[:, :, None], (heads, chans, 1)).reshape(rows, 1)
        state = kept * state + added
        run_ref[:, span] = base + run
        base = base + last
    s_ref[...] = state.reshape(heads, chans, states)


def mixer_from_zero(valid, x, b, c, dt, rates, gains):
    heads, chans, total = x.shape
    groups, states, _ = b.shape
    per = heads // groups
    return pl.pallas_call(
        mixer_kernel,
        grid=(groups,),
        in_specs=[
            scalar,
            pl.BlockSpec((per, chans, total), lambda g: (g, 0, 0)),
            pl.BlockSpec((1, states, total), lambda g: (g, 0, 0)),
            pl.BlockSpec((1, states, total), lambda g: (g, 0, 0)),
            pl.BlockSpec((per, total), lambda g: (g, 0)),
            pl.BlockSpec((1, heads), lambda g: (0, 0)),
            pl.BlockSpec((1, heads), lambda g: (0, 0)),
        ],
        out_specs=[
            pl.BlockSpec((per, chans, total), lambda g: (g, 0, 0)),
            pl.BlockSpec((per, chans, states), lambda g: (g, 0, 0)),
            pl.BlockSpec((per, total), lambda g: (g, 0)),
        ],
        out_shape=[
            jax.ShapeDtypeStruct((heads, chans, total), jnp.float32),
            jax.ShapeDtypeStruct((heads, chans, states), jnp.float32),
            jax.ShapeDtypeStruct((heads, total), jnp.float32),
        ],
        compiler_params=params(16),
        cost_estimate=pl.CostEstimate(flops=1, bytes_accessed=1, transcendentals=0),
        name="mixer_from_zero",
    )(valid, x, b, c, dt, rates[None], gains[None])


def saved_kernel(kinds, valid_ref, chosen_ref, *refs):
    refs = refs[1:]
    slabs = refs[:kinds]
    y_ref, s_ref, run_ref, c_ref, out_ref, final_ref, done_ref, start, mixed, final, sems = refs[
        kinds:
    ]
    done_ref[...] = jnp.zeros(done_ref.shape, jnp.float32)
    heads, chans, total = y_ref.shape
    groups, states, _ = c_ref.shape
    per = heads // groups
    copies = []
    chosen = jnp.max(chosen_ref[0].astype(jnp.float32))
    for kind in range(kinds):

        @pl.when(chosen == kind)
        def _():
            start[...] = slabs[kind][:heads]

    live = lax.broadcasted_iota(jnp.int32, (1, 1, total), 2) < valid_ref[0]
    some = per // 2
    for part in range(2 * groups):
        group = part // 2
        mine = slice(part * some, (part + 1) * some)
        saved = start[mine]
        fade = jnp.exp(run_ref[mine, :])
        read = jnp.dot(
            saved.reshape(some * chans, states), c_ref[group], preferred_element_type=jnp.float32
        ).reshape(some, chans, total)
        result = y_ref[mine] + fade[:, None, :] * read
        mixed[mine] = jnp.where(live, result, 0.0).astype(jnp.bfloat16)
        kept = fade[:, None, total - 1 :]
        final[mine] = s_ref[mine] + kept * saved.astype(jnp.float32)
        span = pl.ds(part * some, some)
        for held, target in ((mixed, out_ref), (final, final_ref)):
            copies.append(
                pltpu.make_async_copy(held.at[span], target.at[span], sems.at[len(copies)])
            )
            copies[-1].start()
    for copy in copies:
        copy.wait()


def add_saved(after, valid, chosen, slabs, y, s, run, c):
    heads, chans, total = y.shape
    groups, states, _ = c.shape
    return pl.pallas_call(
        functools.partial(saved_kernel, len(slabs)),
        in_specs=[scalar, whole, outside] + [whole] * (len(slabs) + 4),
        out_specs=[distant, distant, whole],
        out_shape=[
            jax.ShapeDtypeStruct((heads, chans, total), jnp.bfloat16),
            jax.ShapeDtypeStruct((heads, chans, states), jnp.float32),
            jax.ShapeDtypeStruct((8, 128), jnp.float32),
        ],
        scratch_shapes=[
            pltpu.VMEM((heads, chans, states), jnp.bfloat16),
            pltpu.VMEM((heads, chans, total), jnp.bfloat16),
            pltpu.VMEM((heads, chans, states), jnp.float32),
            pltpu.SemaphoreType.DMA((4 * groups,)),
        ],
        compiler_params=params(12),
        cost_estimate=pl.CostEstimate(flops=1, bytes_accessed=1, transcendentals=0),
        name="add_saved",
    )(valid, chosen, after, *slabs, y, s, run, c)


def attend_kernel(counts, head, sides, padding, *refs):
    if head == 0:
        seen_ref, table_refs, refs = refs[0], refs[1:3], refs[3:]
    else:
        hidden_ref, chosen_ref, refs = refs[0], refs[1], refs[2:]
    refs = refs[1:]
    q_refs, turn_refs, refs = refs[: len(sides)], refs[len(sides) : len(sides) + 2], refs[len(sides) + 2 :]
    if padding:
        state_ref, refs = refs[0], refs[1:]
    kinds = len(counts)
    kv_refs = ([], [])
    for side in range(2):
        for count in counts:
            kv_refs[side].append(refs[:count])
            refs = refs[count:]
    out_refs = {}
    for asked in sides:
        out_refs[asked], refs = refs[0], refs[1:]
        if asked == 0:
            l_ref, refs = refs[0], refs[1:]
    if padding:
        padded_ref, refs = refs[0], refs[1:]
        mine = lax.axis_index("pool") * state_ref.shape[0]
        for slot in range(state_ref.shape[0]):
            padded_ref[table_refs[0][0, mine + slot] % OWNER] = state_ref[slot]
        padded_ref[-padding:] = state_ref[:padding]
    if head == 0:
        hidden_ref, chosen_ref, refs = refs[0], refs[1], refs[2:]
    keys, turn_keys, values = refs
    pages, page = keys.shape[0] // 2, keys.shape[1]
    rows = q_refs[0].shape[0]
    history = pages * page
    width = PER_GROUP * HEAD_DIM
    segment = lax.axis_index("ctx")
    numbers = (segment, segment ^ 1)
    columns = slice(head * HEAD_DIM, (head + 1) * HEAD_DIM)
    if head == 0:
        found = [locate(kinds, table_refs[side], pages) for side in range(2)]
        chosen = [kind for kind, _ in found]
        for side in range(2):
            chosen_ref[side] = jnp.full(chosen_ref.shape[1:], chosen[side], jnp.int32).astype(
                jnp.bfloat16
            )
    else:
        chosen = [0, 0]

    def read_pages(side, kind):
        sources = kv_refs[side][kind]
        lanes = columns if sources[0].shape[-1] > HEAD_DIM else slice(0, HEAD_DIM)
        if len(sources) == 1:
            return [sources[0][:pages, half, :, lanes] for half in range(2)]
        return [sources[half][:pages, :, lanes] for half in range(2)]

    def take_pages(side, kind):
        for place, taken in zip((keys, values), read_pages(side, kind)):
            place[side * pages : (side + 1) * pages, :, :HEAD_DIM] = taken

    for side in range(2):
        if head and kinds == 2:
            first_one, other = (read_pages(side, kind) for kind in range(2))
            target = slice(side * pages, (side + 1) * pages)
            weight = chosen_ref[side][:1][None]
            for half, place in enumerate((keys, values)):
                place[target, :, :HEAD_DIM] = first_one[half] * (1 - weight) + other[half] * weight
        else:
            for kind in range(kinds):

                @pl.when(chosen[side] == kind)
                def _():
                    take_pages(side, kind)

    if head == 0:
        in_page = lax.broadcasted_iota(jnp.int32, (page, HEAD_DIM), 0)
        seen = seen_ref[0]
        for side in range(2):
            start = numbers[side] * history
            for number in range(pages):
                left = seen - start - (table_refs[side][0, found[side][1] + number] % OWNER) * page
                hidden_ref[side * pages + number] = jnp.where(in_page < left, 0.0, HIDDEN).astype(
                    jnp.bfloat16
                )
    keys[:, :, HEAD_DIM:] = hidden_ref[...]
    values[:, :, HEAD_DIM:] = jnp.ones(
        (values.shape[0], page, HEAD_DIM), jnp.bfloat16
    )
    first = lax.broadcasted_iota(jnp.int32, (rows, rows), 0)
    second = lax.broadcasted_iota(jnp.int32, (rows, rows), 1)
    eye = jnp.where(first == second, 1.0, 0.0).astype(jnp.bfloat16)
    for i, asked in enumerate(sides):
        asking = segment ^ (2 * asked)
        for side in range(2):
            ahead = first + numbers[side] * rows
            turn_keys[i, pl.ds(side * rows, rows), HEAD_DIM:] = jnp.where(
                ahead <= second + asking * rows, 0.0, HIDDEN
            ).astype(jnp.bfloat16)
    turn_pages = rows // page
    for side in range(2):
        for i in range(len(sides)):
            turn_keys[i, pl.ds(side * rows, rows), pl.ds(0, HEAD_DIM)] = turn_refs[side][0, :, columns]
        values[
            pl.ds(2 * pages + side * turn_pages, turn_pages), :, pl.ds(0, HEAD_DIM)
        ] = turn_refs[side][1, :, columns].reshape(turn_pages, page, HEAD_DIM)
    depth = 2 * HEAD_DIM
    all_keys = 2 * history
    lane = lax.broadcasted_iota(jnp.int32, (rows, HEAD_DIM), 1)
    across = (((1,), (1,)), ((), ()))
    at_once = 2
    for which, asked in enumerate(sides):
        out_ref = out_refs[asked]
        stats = jnp.zeros((rows, HEAD_DIM), jnp.float32)
        for batch in range(PER_GROUP // at_once):
            asks = jnp.concatenate(
                [
                    jnp.concatenate(
                        [
                            q_refs[which][:, pl.ds(head * width + (batch * at_once + i) * HEAD_DIM, HEAD_DIM)],
                            eye,
                        ],
                        axis=1,
                    )
                    for i in range(at_once)
                ],
                axis=0,
            )
            peak = summed = None
            for low in range(0, all_keys, CHUNK):
                high = min(low + CHUNK, all_keys)
                scores = lax.dot_general(
                    asks,
                    keys[...].reshape(all_keys, depth)[low:high],
                    across,
                    preferred_element_type=jnp.float32,
                )
                if high == all_keys:
                    new = lax.dot_general(
                        asks, turn_keys[which], across, preferred_element_type=jnp.float32
                    )
                    scores = jnp.concatenate([scores, new], axis=1)
                    high = high + 2 * rows
                top = jnp.max(scores, axis=1, keepdims=True)
                if peak is not None:
                    top = jnp.maximum(top, peak)
                weights = jnp.exp2((scores - top) * TO_POWER).astype(jnp.bfloat16)
                added = jnp.dot(
                    weights,
                    values[...].reshape(all_keys + 2 * rows, depth)[low:high],
                    preferred_element_type=jnp.float32,
                )
                if peak is not None:
                    added = added + summed * jnp.exp2((peak - top) * TO_POWER)
                peak, summed = top, added
            totals = summed[:, HEAD_DIM:]
            mixed = (summed[:, :HEAD_DIM] / totals).astype(jnp.bfloat16)
            level = peak * TO_POWER + jnp.log2(totals)
            span = pl.ds(batch * at_once * rows, at_once * rows)
            out_ref[span] = mixed
            for i in range(at_once):
                stats = jnp.where(
                    lane == batch * at_once + i, level[i * rows : (i + 1) * rows], stats
                )
        stats = stats.T[:PER_GROUP]
        if asked:
            high = stats.astype(jnp.bfloat16).astype(jnp.float32)
            middle = (stats - high).astype(jnp.bfloat16).astype(jnp.float32)
            low = stats - high - middle
            spare = out_ref.shape[0] - PER_GROUP * rows - STAT_ROWS
            if spare:
                out_ref[pl.ds(PER_GROUP * rows + STAT_ROWS, spare)] = jnp.zeros(
                    (spare, HEAD_DIM), jnp.bfloat16
                )
            out_ref[pl.ds(PER_GROUP * rows, STAT_ROWS)] = jnp.concatenate(
                [high, middle, low, jnp.zeros_like(low)], axis=0
            ).astype(jnp.bfloat16)
        else:
            l_ref[...] = stats


def attend(head, sides, pages, marks, after, queries, own_kv, partner_kv, turns, states=None):
    rows = queries[0].shape[0]
    page = own_kv[0][0].shape[-2]
    counts = tuple(len(choice) for choice in own_kv)
    flat = [array for choice in (*own_kv, *partner_kv) for array in choice]
    all_rows = PER_GROUP * rows
    shapes = []
    for asked in sides:
        extra = STAT_ROWS + (SPARE_ROWS if len(sides) == 2 else 0) if asked else 0
        shapes.append(jax.ShapeDtypeStruct((all_rows + extra, HEAD_DIM), jnp.bfloat16))
        if not asked:
            shapes.append(jax.ShapeDtypeStruct((PER_GROUP, rows), jnp.float32))
    asks = [queries[asked] for asked in sides]
    padding = 0
    if states is not None:
        padding = 2
        flat = [states] + flat
        shapes.append(
            jax.ShapeDtypeStruct((states.shape[0] + padding,) + states.shape[1:], states.dtype)
        )
    if head == 0:
        shapes.append(jax.ShapeDtypeStruct((2 * pages, page, HEAD_DIM), jnp.bfloat16))
        shapes.append(jax.ShapeDtypeStruct((2, 16, 128), jnp.bfloat16))
    return pl.pallas_call(
        functools.partial(attend_kernel, counts, head, sides, padding),
        in_specs=([scalar] * 3 if head == 0 else [whole] * 2) + [outside] + [whole] * (2 + len(sides) + len(flat)),
        out_specs=[whole] * len(shapes),
        out_shape=shapes,
        scratch_shapes=[
            pltpu.VMEM((2 * pages, page, 2 * HEAD_DIM), jnp.bfloat16),
            pltpu.VMEM((len(sides), 2 * rows, 2 * HEAD_DIM), jnp.bfloat16),
            pltpu.VMEM((2 * pages + 2 * rows // page, page, 2 * HEAD_DIM), jnp.bfloat16),
        ],
        compiler_params=params(24),
        cost_estimate=pl.CostEstimate(flops=1, bytes_accessed=1, transcendentals=0),
        name=f"attend_{head}_{len(sides)}_{sides[0]}",
    )(*marks, after, *asks, *turns, *flat)


def merge_kernel(head, valid_ref, after_ref, o_ref, l_ref, got_ref, *refs):
    out_ref, held, sem = refs[-3:]
    rows, width = held.shape
    place = lax.axis_index("ctx") * rows + lax.broadcasted_iota(jnp.int32, (rows, HEAD_DIM), 0)
    live = place < valid_ref[0]
    parts = got_ref[pl.ds(PER_GROUP * rows, STAT_ROWS)].astype(jnp.float32)
    level = parts[:PER_GROUP] + parts[PER_GROUP : 2 * PER_GROUP]
    level = level + parts[2 * PER_GROUP : 3 * PER_GROUP]
    share = 1.0 / (1.0 + jnp.exp2(level - l_ref[...]))
    share = jnp.concatenate([share, jnp.zeros((rows - PER_GROUP, rows), jnp.float32)], axis=0).T
    copies = []
    for member in range(PER_GROUP):
        span = pl.ds(member * rows, rows)
        here = o_ref[span].astype(jnp.float32)
        there = got_ref[span].astype(jnp.float32)
        result = there + share[:, member : member + 1] * (here - there)
        lanes = pl.ds(member * HEAD_DIM, HEAD_DIM)
        held[:, lanes] = jnp.where(live, result, 0.0).astype(jnp.bfloat16)
        if member % 4 == 3:
            first = (member - 3) * HEAD_DIM
            copies.append(
                pltpu.make_async_copy(
                    held.at[:, pl.ds(first, 4 * HEAD_DIM)],
                    out_ref.at[:, pl.ds(head * width + first, 4 * HEAD_DIM)],
                    sem.at[member // 4],
                )
            )
            copies[-1].start()
    for copy in copies:
        copy.wait()


def merge(head, heads, after, valid, part, rows, before=None):
    width = PER_GROUP * HEAD_DIM
    extra = [] if before is None else [before]
    return pl.pallas_call(
        functools.partial(merge_kernel, head),
        in_specs=[scalar, outside] + [whole] * len(part) + [distant] * len(extra),
        out_specs=distant,
        out_shape=jax.ShapeDtypeStruct((rows, heads * width), jnp.bfloat16),
        input_output_aliases={2 + len(part): 0} if extra else {},
        scratch_shapes=[
            pltpu.VMEM((rows, width), jnp.bfloat16),
            pltpu.SemaphoreType.DMA((PER_GROUP // 4,)),
        ],
        compiler_params=params(8),
        name=f"merge_{head}",
    )(valid, after, *part, *extra)


def route_blocks(kv_local, state_local, owner_row, index_row):
    parties = lax.axis_size("pool")
    myself = lax.axis_index("pool")
    pages = kv_local.shape[0]
    capacity = max(1, 2 * pages // parties)
    sessions = jnp.arange(parties, dtype=jnp.int32)
    table = (
        (owner_row[:, None] == sessions[None, :]).astype(jnp.int32).reshape(parties, pages, parties)
    )
    before = jnp.cumsum(table, axis=1) - table
    ranks = jnp.sum(before * table, axis=2)
    owners = owner_row.reshape(parties, pages)
    my_owner = lax.dynamic_index_in_dim(owners, myself, 0, keepdims=False)
    device_rank = lax.dynamic_index_in_dim(ranks, myself, 0, keepdims=False)

    def spread(array):
        empty = jnp.zeros((parties, capacity) + array.shape[1:], array.dtype)
        sent = empty.at[my_owner, device_rank].set(array)
        return lax.all_to_all(sent, "pool", split_axis=0, concat_axis=0, tiled=True)

    got_kv, got_state = spread(kv_local), spread(state_local)
    flat_place = (sessions[:, None] * capacity + ranks).reshape(-1)
    target = jnp.where(owner_row == myself, index_row, pages)
    where_from = jnp.zeros((pages,), jnp.int32).at[target].set(flat_place, mode="drop")
    return (
        got_kv.reshape((parties * capacity,) + kv_local.shape[1:])[where_from],
        got_state.reshape((parties * capacity,) + state_local.shape[1:])[where_from],
    )


def local(
    kv_pool,
    state_pool,
    block_owner,
    block_index,
    history_len,
    turn_len,
    mixer_in,
    input_proj,
    output_proj,
    step_size,
    decay_rate,
    bypass_factor,
    queries,
    turn_kv,
):
    parties = lax.axis_size("pool")
    segments = lax.axis_size("ctx")
    kv = kv_pool[0]
    pages = kv.shape[0]
    rows = queries.shape[1]
    heads = kv.shape[-1] // HEAD_DIM
    partner = [(i, i ^ 1) for i in range(segments)]
    opposite = [(i, i ^ 2) for i in range(segments)]

    def to_partner(array):
        return lax.ppermute(array, "ctx", partner)

    def to_opposite(array):
        return lax.ppermute(array, "ctx", opposite)

    if parties == 2:
        swap = [(0, 1), (1, 0)]
        moved, pieces, rest = [], [], kv
        for head in range(heads):
            columns = slice(head * HEAD_DIM, (head + 1) * HEAD_DIM)
            cut = rest[..., columns]
            if head:
                cut = jnp.concatenate([cut, cut[:1]], axis=0)
            cut = (cut,)
            cut, rest = lax.optimization_barrier((cut, rest))
            pieces.append(cut)
            moved.append(tuple(lax.ppermute(piece, "pool", swap) for piece in cut))
        table = block_owner * OWNER + block_index
    else:
        table = jnp.arange(pages, dtype=jnp.int32)[None]
        routed, slab = route_blocks(kv, state_pool, block_owner[0], block_index[0])
        moved = [(routed[..., h * HEAD_DIM : (h + 1) * HEAD_DIM],) for h in range(heads)]
    asks = (queries[0], to_opposite(queries[0]))

    turns = (turn_kv[0], to_partner(turn_kv[0]))
    tables = (table, to_partner(table))
    y, s, run = mixer_from_zero(
        turn_len, mixer_in[0], input_proj[0], output_proj[0], step_size[0], decay_rate, bypass_factor
    )
    parts = []
    after = run
    marks = (history_len, *tables)
    for head in range(heads):
        came, after = lax.optimization_barrier((moved[head], after))
        own_kv, partner_kv = (came,), (tuple(to_partner(piece) for piece in came),)
        if parties == 2:
            beside = tuple(to_partner(piece) for piece in pieces[head])
            own_kv, partner_kv = (pieces[head],) + own_kv, (beside,) + partner_kv
        ask = functools.partial(
            attend,
            head,
            pages=pages,
            marks=marks,
            queries=asks,
            own_kv=own_kv,
            partner_kv=partner_kv,
            turns=turns,
        )
        if head + 1 < heads:
            states = state_pool if parties == 2 and head == 0 else None
            sent, o, after, *padded, hidden, chosen = ask(sides=(1, 0), after=after, states=states)
            marks = (hidden, chosen)
            if padded:
                ordered = padded[0]
                slab = lax.ppermute(ordered, "pool", swap)
        else:
            (sent,) = ask(sides=(1,), after=after)
            o, after = ask(sides=(0,), after=sent)
        parts.append((o, after, to_opposite(sent)))
    slab, after = lax.optimization_barrier((slab, after))
    slabs = (ordered, slab) if parties == 2 else (slab,)
    mixed, final, after = add_saved(after, turn_len, chosen, slabs, y, s, run, output_proj[0])
    attended = None
    for head in range(heads):
        attended = merge(head, heads, after, turn_len, parts[head], rows, attended)
    return (mixed[None], final[None], attended[None])


def solution(mesh):
    return jax.shard_map(
        local,
        mesh=mesh,
        in_specs=(
            P("ctx", "pool", None, None, "head"),
            P("pool", "ctx", "head"),
            P("ctx", None),
            P("ctx", None),
            P("pool"),
            P("pool"),
            P("pool", "head", "ctx", None),
            P("pool", "head", None, None),
            P("pool", "head", None, None),
            P("pool", "head", None),
            P("head"),
            P("head"),
            P("pool", "ctx", "head"),
            P("pool", None, "ctx", "head"),
        ),
        out_specs=(
            P("pool", "head", "ctx", None),
            P("pool", "head", "ctx", None),
            P("pool", "ctx", "head"),
        ),
        check_vma=False,
    )
```

```python
import functools

import jax
import jax.numpy as jnp
from jax import lax
from jax.experimental import pallas as pl
from jax.experimental.pallas import tpu as pltpu
from jax.sharding import PartitionSpec as P

Q_HEADS = 64
KV_HEADS = 8
HEAD_DIM = 128
PER_GROUP = Q_HEADS // KV_HEADS
BLK = 128
HIDDEN = -1e30
TO_POWER = (HEAD_DIM**-0.5) * 1.4426950408889634
STAT_ROWS = 32
SPARE_ROWS = 16
CHUNK = 768
OWNER = 65536

whole = pl.BlockSpec(memory_space=pltpu.VMEM)
scalar = pl.BlockSpec(memory_space=pltpu.SMEM)
outside = pl.BlockSpec(memory_space=pl.ANY)
distant = pl.BlockSpec(memory_space=pltpu.HBM)


def params(mib):
    return pltpu.CompilerParams(vmem_limit_bytes=mib * 2**20)


def locate(kinds, table_ref, pages):
    if kinds == 1:
        return 0, 0
    myself = lax.axis_index("pool")
    kind = jnp.where(table_ref[0, myself * pages] // OWNER == myself, 0, 1).astype(jnp.int32)
    return kind, jnp.where(kind == 0, myself, 1 - myself) * pages


def as_column(row_ref, start, count):
    row = jnp.broadcast_to(row_ref[...], (count, row_ref.shape[1]))
    across = lax.broadcasted_iota(jnp.int32, row.shape, 1)
    down = lax.broadcasted_iota(jnp.int32, row.shape, 0)
    return jnp.sum(jnp.where(across == down + start, row, 0.0), axis=1, keepdims=True)


def mixer_kernel(valid_ref, x_ref, b_ref, c_ref, dt_ref, rate_ref, gain_ref, y_ref, s_ref, run_ref):
    heads, chans, total = x_ref.shape
    start = pl.program_id(0) * heads
    states = b_ref.shape[1]
    rows = heads * chans
    place = lax.broadcasted_iota(jnp.int32, (heads, total), 1)
    steps = jnp.where(place < valid_ref[0], dt_ref[...], 0.0)
    falls = -as_column(rate_ref, start, heads) * steps
    gains = as_column(gain_ref, start, heads)
    first = lax.broadcasted_iota(jnp.int32, (BLK, BLK), 0)
    second = lax.broadcasted_iota(jnp.int32, (BLK, BLK), 1)
    upper = first <= second
    ones_upper = jnp.where(upper, 1.0, 0.0).astype(jnp.float32)
    turned = b_ref[0].T
    state = jnp.zeros((rows, states), jnp.float32)
    base = jnp.zeros((heads, 1), jnp.float32)
    for blk in range(total // BLK):
        span = slice(blk * BLK, (blk + 1) * BLK)
        run = jnp.dot(
            falls[:, span],
            ones_upper,
            precision=lax.Precision.HIGHEST,
            preferred_element_type=jnp.float32,
        )
        run_col = run.T
        last = run[:, BLK - 1 :]
        pairs = jnp.dot(turned[span], c_ref[0, :, span], preferred_element_type=jnp.float32)
        pairs = jnp.where(upper, pairs, 0.0)
        x_blk = x_ref[:, :, span].astype(jnp.float32)
        stepped = (x_blk * steps[:, None, span]).astype(jnp.bfloat16)
        inside = []
        for head in range(heads):
            gap = jnp.minimum(run[head : head + 1, :] - run_col[:, head : head + 1], 0.0)
            mixing = (jnp.exp(gap) * pairs).astype(jnp.bfloat16)
            inside.append(jnp.dot(stepped[head], mixing, preferred_element_type=jnp.float32))
        result = jnp.stack(inside) + gains[:, :, None] * x_blk
        if blk:
            read = jnp.dot(
                state.astype(jnp.bfloat16), c_ref[0, :, span], preferred_element_type=jnp.float32
            )
            result = result + jnp.exp(run)[:, None, :] * read.reshape(heads, chans, BLK)
        y_ref[:, :, span] = result
        weights = jnp.exp(last - run) * steps[:, span]
        weighted = (x_blk * weights[:, None, :]).astype(jnp.bfloat16).reshape(rows, BLK)
        added = jnp.dot(weighted, turned[span], preferred_element_type=jnp.float32)
        kept = jnp.broadcast_to(jnp.exp(last)[:, :, None], (heads, chans, 1)).reshape(rows, 1)
        state = kept * state + added
        run_ref[:, span] = base + run
        base = base + last
    s_ref[...] = state.reshape(heads, chans, states)


def mixer_from_zero(valid, x, b, c, dt, rates, gains):
    heads, chans, total = x.shape
    groups, states, _ = b.shape
    per = heads // groups
    return pl.pallas_call(
        mixer_kernel,
        grid=(groups,),
        in_specs=[
            scalar,
            pl.BlockSpec((per, chans, total), lambda g: (g, 0, 0)),
            pl.BlockSpec((1, states, total), lambda g: (g, 0, 0)),
            pl.BlockSpec((1, states, total), lambda g: (g, 0, 0)),
            pl.BlockSpec((per, total), lambda g: (g, 0)),
            pl.BlockSpec((1, heads), lambda g: (0, 0)),
            pl.BlockSpec((1, heads), lambda g: (0, 0)),
        ],
        out_specs=[
            pl.BlockSpec((per, chans, total), lambda g: (g, 0, 0)),
            pl.BlockSpec((per, chans, states), lambda g: (g, 0, 0)),
            pl.BlockSpec((per, total), lambda g: (g, 0)),
        ],
        out_shape=[
            jax.ShapeDtypeStruct((heads, chans, total), jnp.float32),
            jax.ShapeDtypeStruct((heads, chans, states), jnp.float32),
            jax.ShapeDtypeStruct((heads, total), jnp.float32),
        ],
        compiler_params=params(16),
        cost_estimate=pl.CostEstimate(flops=1, bytes_accessed=1, transcendentals=0),
        name="mixer_from_zero",
    )(valid, x, b, c, dt, rates[None], gains[None])


def saved_kernel(kinds, valid_ref, chosen_ref, *refs):
    refs = refs[1:]
    slabs = refs[:kinds]
    y_ref, s_ref, run_ref, c_ref, out_ref, final_ref, done_ref, start, mixed, final, sems = refs[
        kinds:
    ]
    done_ref[...] = jnp.zeros(done_ref.shape, jnp.float32)
    heads, chans, total = y_ref.shape
    groups, states, _ = c_ref.shape
    per = heads // groups
    copies = []
    chosen = jnp.max(chosen_ref[0].astype(jnp.float32))
    for kind in range(kinds):

        @pl.when(chosen == kind)
        def _():
            start[...] = slabs[kind][:heads]

    live = lax.broadcasted_iota(jnp.int32, (1, 1, total), 2) < valid_ref[0]
    some = per // 2
    for part in range(2 * groups):
        group = part // 2
        mine = slice(part * some, (part + 1) * some)
        saved = start[mine]
        fade = jnp.exp(run_ref[mine, :])
        read = jnp.dot(
            saved.reshape(some * chans, states), c_ref[group], preferred_element_type=jnp.float32
        ).reshape(some, chans, total)
        result = y_ref[mine] + fade[:, None, :] * read
        mixed[mine] = jnp.where(live, result, 0.0).astype(jnp.bfloat16)
        kept = fade[:, None, total - 1 :]
        final[mine] = s_ref[mine] + kept * saved.astype(jnp.float32)
        span = pl.ds(part * some, some)
        for held, target in ((mixed, out_ref), (final, final_ref)):
            copies.append(
                pltpu.make_async_copy(held.at[span], target.at[span], sems.at[len(copies)])
            )
            copies[-1].start()
    for copy in copies:
        copy.wait()


def add_saved(after, valid, chosen, slabs, y, s, run, c):
    heads, chans, total = y.shape
    groups, states, _ = c.shape
    return pl.pallas_call(
        functools.partial(saved_kernel, len(slabs)),
        in_specs=[scalar, whole, outside] + [whole] * (len(slabs) + 4),
        out_specs=[distant, distant, whole],
        out_shape=[
            jax.ShapeDtypeStruct((heads, chans, total), jnp.bfloat16),
            jax.ShapeDtypeStruct((heads, chans, states), jnp.float32),
            jax.ShapeDtypeStruct((8, 128), jnp.float32),
        ],
        scratch_shapes=[
            pltpu.VMEM((heads, chans, states), jnp.bfloat16),
            pltpu.VMEM((heads, chans, total), jnp.bfloat16),
            pltpu.VMEM((heads, chans, states), jnp.float32),
            pltpu.SemaphoreType.DMA((4 * groups,)),
        ],
        compiler_params=params(12),
        cost_estimate=pl.CostEstimate(flops=1, bytes_accessed=1, transcendentals=0),
        name="add_saved",
    )(valid, chosen, after, *slabs, y, s, run, c)


def attend_kernel(counts, head, sides, padding, *refs):
    if head == 0:
        seen_ref, table_refs, refs = refs[0], refs[1:3], refs[3:]
    else:
        hidden_ref, chosen_ref, refs = refs[0], refs[1], refs[2:]
    refs = refs[1:]
    q_refs, turn_refs, refs = refs[: len(sides)], refs[len(sides) : len(sides) + 2], refs[len(sides) + 2 :]
    if padding:
        state_ref, refs = refs[0], refs[1:]
    kinds = len(counts)
    kv_refs = ([], [])
    for side in range(2):
        for count in counts:
            kv_refs[side].append(refs[:count])
            refs = refs[count:]
    out_refs = {}
    for asked in sides:
        out_refs[asked], refs = refs[0], refs[1:]
        if asked == 0:
            l_ref, refs = refs[0], refs[1:]
    if padding:
        padded_ref, refs = refs[0], refs[1:]
        mine = lax.axis_index("pool") * state_ref.shape[0]
        for slot in range(state_ref.shape[0]):
            padded_ref[table_refs[0][0, mine + slot] % OWNER] = state_ref[slot]
        padded_ref[-padding:] = state_ref[:padding]
    if head == 0:
        hidden_ref, chosen_ref, refs = refs[0], refs[1], refs[2:]
    keys, turn_keys, values = refs
    pages, page = keys.shape[0] // 2, keys.shape[1]
    rows = q_refs[0].shape[0]
    history = pages * page
    width = PER_GROUP * HEAD_DIM
    segment = lax.axis_index("ctx")
    numbers = (segment, segment ^ 1)
    columns = slice(head * HEAD_DIM, (head + 1) * HEAD_DIM)
    if head == 0:
        found = [locate(kinds, table_refs[side], pages) for side in range(2)]
        chosen = [kind for kind, _ in found]
        for side in range(2):
            chosen_ref[side] = jnp.full(chosen_ref.shape[1:], chosen[side], jnp.int32).astype(
                jnp.bfloat16
            )
    else:
        chosen = [0, 0]

    def read_pages(side, kind):
        sources = kv_refs[side][kind]
        lanes = columns if sources[0].shape[-1] > HEAD_DIM else slice(0, HEAD_DIM)
        if len(sources) == 1:
            return [sources[0][:pages, half, :, lanes] for half in range(2)]
        return [sources[half][:pages, :, lanes] for half in range(2)]

    def take_pages(side, kind):
        for place, taken in zip((keys, values), read_pages(side, kind)):
            place[side * pages : (side + 1) * pages, :, :HEAD_DIM] = taken

    for side in range(2):
        if head and kinds == 2:
            first_one, other = (read_pages(side, kind) for kind in range(2))
            target = slice(side * pages, (side + 1) * pages)
            weight = chosen_ref[side][:1][None]
            for half, place in enumerate((keys, values)):
                place[target, :, :HEAD_DIM] = first_one[half] * (1 - weight) + other[half] * weight
        else:
            for kind in range(kinds):

                @pl.when(chosen[side] == kind)
                def _():
                    take_pages(side, kind)

    if head == 0:
        in_page = lax.broadcasted_iota(jnp.int32, (page, HEAD_DIM), 0)
        seen = seen_ref[0]
        for side in range(2):
            start = numbers[side] * history
            for number in range(pages):
                left = seen - start - (table_refs[side][0, found[side][1] + number] % OWNER) * page
                hidden_ref[side * pages + number] = jnp.where(in_page < left, 0.0, HIDDEN).astype(
                    jnp.bfloat16
                )
    keys[:, :, HEAD_DIM:] = hidden_ref[...]
    values[:, :, HEAD_DIM:] = jnp.ones(
        (values.shape[0], page, HEAD_DIM), jnp.bfloat16
    )
    first = lax.broadcasted_iota(jnp.int32, (rows, rows), 0)
    second = lax.broadcasted_iota(jnp.int32, (rows, rows), 1)
    eye = jnp.where(first == second, 1.0, 0.0).astype(jnp.bfloat16)
    for i, asked in enumerate(sides):
        asking = segment ^ (2 * asked)
        for side in range(2):
            ahead = first + numbers[side] * rows
            turn_keys[i, pl.ds(side * rows, rows), HEAD_DIM:] = jnp.where(
                ahead <= second + asking * rows, 0.0, HIDDEN
            ).astype(jnp.bfloat16)
    turn_pages = rows // page
    for side in range(2):
        for i in range(len(sides)):
            turn_keys[i, pl.ds(side * rows, rows), pl.ds(0, HEAD_DIM)] = turn_refs[side][0, :, columns]
        values[
            pl.ds(2 * pages + side * turn_pages, turn_pages), :, pl.ds(0, HEAD_DIM)
        ] = turn_refs[side][1, :, columns].reshape(turn_pages, page, HEAD_DIM)
    depth = 2 * HEAD_DIM
    all_keys = 2 * history
    lane = lax.broadcasted_iota(jnp.int32, (rows, HEAD_DIM), 1)
    across = (((1,), (1,)), ((), ()))
    at_once = 2
    for which, asked in enumerate(sides):
        out_ref = out_refs[asked]
        stats = jnp.zeros((rows, HEAD_DIM), jnp.float32)
        for batch in range(PER_GROUP // at_once):
            asks = jnp.concatenate(
                [
                    jnp.concatenate(
                        [
                            q_refs[which][:, pl.ds(head * width + (batch * at_once + i) * HEAD_DIM, HEAD_DIM)],
                            eye,
                        ],
                        axis=1,
                    )
                    for i in range(at_once)
                ],
                axis=0,
            )
            peak = summed = None
            for low in range(0, all_keys, CHUNK):
                high = min(low + CHUNK, all_keys)
                scores = lax.dot_general(
                    asks,
                    keys[...].reshape(all_keys, depth)[low:high],
                    across,
                    preferred_element_type=jnp.float32,
                )
                if high == all_keys:
                    new = lax.dot_general(
                        asks, turn_keys[which], across, preferred_element_type=jnp.float32
                    )
                    scores = jnp.concatenate([scores, new], axis=1)
                    high = high + 2 * rows
                top = jnp.max(scores, axis=1, keepdims=True)
                if peak is not None:
                    top = jnp.maximum(top, peak)
                weights = jnp.exp2((scores - top) * TO_POWER).astype(jnp.bfloat16)
                added = jnp.dot(
                    weights,
                    values[...].reshape(all_keys + 2 * rows, depth)[low:high],
                    preferred_element_type=jnp.float32,
                )
                if peak is not None:
                    added = added + summed * jnp.exp2((peak - top) * TO_POWER)
                peak, summed = top, added
            totals = summed[:, HEAD_DIM:]
            mixed = (summed[:, :HEAD_DIM] / totals).astype(jnp.bfloat16)
            level = peak * TO_POWER + jnp.log2(totals)
            span = pl.ds(batch * at_once * rows, at_once * rows)
            out_ref[span] = mixed
            for i in range(at_once):
                stats = jnp.where(
                    lane == batch * at_once + i, level[i * rows : (i + 1) * rows], stats
                )
        stats = stats.T[:PER_GROUP]
        if asked:
            high = stats.astype(jnp.bfloat16).astype(jnp.float32)
            middle = (stats - high).astype(jnp.bfloat16).astype(jnp.float32)
            low = stats - high - middle
            spare = out_ref.shape[0] - PER_GROUP * rows - STAT_ROWS
            if spare:
                out_ref[pl.ds(PER_GROUP * rows + STAT_ROWS, spare)] = jnp.zeros(
                    (spare, HEAD_DIM), jnp.bfloat16
                )
            out_ref[pl.ds(PER_GROUP * rows, STAT_ROWS)] = jnp.concatenate(
                [high, middle, low, jnp.zeros_like(low)], axis=0
            ).astype(jnp.bfloat16)
        else:
            l_ref[...] = stats


def attend(head, sides, pages, marks, after, queries, own_kv, partner_kv, turns, states=None):
    rows = queries[0].shape[0]
    page = own_kv[0][0].shape[-2]
    counts = tuple(len(choice) for choice in own_kv)
    flat = [array for choice in (*own_kv, *partner_kv) for array in choice]
    all_rows = PER_GROUP * rows
    shapes = []
    for asked in sides:
        extra = STAT_ROWS + (SPARE_ROWS if len(sides) == 2 else 0) if asked else 0
        shapes.append(jax.ShapeDtypeStruct((all_rows + extra, HEAD_DIM), jnp.bfloat16))
        if not asked:
            shapes.append(jax.ShapeDtypeStruct((PER_GROUP, rows), jnp.float32))
    asks = [queries[asked] for asked in sides]
    padding = 0
    if states is not None:
        padding = 1
        flat = [states] + flat
        shapes.append(
            jax.ShapeDtypeStruct((states.shape[0] + padding,) + states.shape[1:], states.dtype)
        )
    if head == 0:
        shapes.append(jax.ShapeDtypeStruct((2 * pages, page, HEAD_DIM), jnp.bfloat16))
        shapes.append(jax.ShapeDtypeStruct((2, 16, 128), jnp.bfloat16))
    return pl.pallas_call(
        functools.partial(attend_kernel, counts, head, sides, padding),
        in_specs=([scalar] * 3 if head == 0 else [whole] * 2) + [outside] + [whole] * (2 + len(sides) + len(flat)),
        out_specs=[whole] * len(shapes),
        out_shape=shapes,
        scratch_shapes=[
            pltpu.VMEM((2 * pages, page, 2 * HEAD_DIM), jnp.bfloat16),
            pltpu.VMEM((len(sides), 2 * rows, 2 * HEAD_DIM), jnp.bfloat16),
            pltpu.VMEM((2 * pages + 2 * rows // page, page, 2 * HEAD_DIM), jnp.bfloat16),
        ],
        compiler_params=params(24),
        cost_estimate=pl.CostEstimate(flops=1, bytes_accessed=1, transcendentals=0),
        name=f"attend_{head}_{len(sides)}_{sides[0]}",
    )(*marks, after, *asks, *turns, *flat)


def merge_kernel(head, valid_ref, after_ref, o_ref, l_ref, got_ref, *refs):
    out_ref, held, sem = refs[-3:]
    rows, width = held.shape
    place = lax.axis_index("ctx") * rows + lax.broadcasted_iota(jnp.int32, (rows, HEAD_DIM), 0)
    live = place < valid_ref[0]
    parts = got_ref[pl.ds(PER_GROUP * rows, STAT_ROWS)].astype(jnp.float32)
    level = parts[:PER_GROUP] + parts[PER_GROUP : 2 * PER_GROUP]
    level = level + parts[2 * PER_GROUP : 3 * PER_GROUP]
    share = 1.0 / (1.0 + jnp.exp2(level - l_ref[...]))
    share = jnp.concatenate([share, jnp.zeros((rows - PER_GROUP, rows), jnp.float32)], axis=0).T
    copies = []
    for member in range(PER_GROUP):
        span = pl.ds(member * rows, rows)
        here = o_ref[span].astype(jnp.float32)
        there = got_ref[span].astype(jnp.float32)
        result = there + share[:, member : member + 1] * (here - there)
        lanes = pl.ds(member * HEAD_DIM, HEAD_DIM)
        held[:, lanes] = jnp.where(live, result, 0.0).astype(jnp.bfloat16)
        if member % 4 == 3:
            first = (member - 3) * HEAD_DIM
            copies.append(
                pltpu.make_async_copy(
                    held.at[:, pl.ds(first, 4 * HEAD_DIM)],
                    out_ref.at[:, pl.ds(head * width + first, 4 * HEAD_DIM)],
                    sem.at[member // 4],
                )
            )
            copies[-1].start()
    for copy in copies:
        copy.wait()


def merge(head, heads, after, valid, part, rows, before=None):
    width = PER_GROUP * HEAD_DIM
    extra = [] if before is None else [before]
    return pl.pallas_call(
        functools.partial(merge_kernel, head),
        in_specs=[scalar, outside] + [whole] * len(part) + [distant] * len(extra),
        out_specs=distant,
        out_shape=jax.ShapeDtypeStruct((rows, heads * width), jnp.bfloat16),
        input_output_aliases={2 + len(part): 0} if extra else {},
        scratch_shapes=[
            pltpu.VMEM((rows, width), jnp.bfloat16),
            pltpu.SemaphoreType.DMA((PER_GROUP // 4,)),
        ],
        compiler_params=params(8),
        name=f"merge_{head}",
    )(valid, after, *part, *extra)


def route_blocks(kv_local, state_local, owner_row, index_row):
    parties = lax.axis_size("pool")
    myself = lax.axis_index("pool")
    pages = kv_local.shape[0]
    capacity = max(1, 2 * pages // parties)
    sessions = jnp.arange(parties, dtype=jnp.int32)
    table = (
        (owner_row[:, None] == sessions[None, :]).astype(jnp.int32).reshape(parties, pages, parties)
    )
    before = jnp.cumsum(table, axis=1) - table
    ranks = jnp.sum(before * table, axis=2)
    owners = owner_row.reshape(parties, pages)
    my_owner = lax.dynamic_index_in_dim(owners, myself, 0, keepdims=False)
    device_rank = lax.dynamic_index_in_dim(ranks, myself, 0, keepdims=False)

    def spread(array):
        empty = jnp.zeros((parties, capacity) + array.shape[1:], array.dtype)
        sent = empty.at[my_owner, device_rank].set(array)
        return lax.all_to_all(sent, "pool", split_axis=0, concat_axis=0, tiled=True)

    got_kv, got_state = spread(kv_local), spread(state_local)
    flat_place = (sessions[:, None] * capacity + ranks).reshape(-1)
    target = jnp.where(owner_row == myself, index_row, pages)
    where_from = jnp.zeros((pages,), jnp.int32).at[target].set(flat_place, mode="drop")
    return (
        got_kv.reshape((parties * capacity,) + kv_local.shape[1:])[where_from],
        got_state.reshape((parties * capacity,) + state_local.shape[1:])[where_from],
    )


def local(
    kv_pool,
    state_pool,
    block_owner,
    block_index,
    history_len,
    turn_len,
    mixer_in,
    input_proj,
    output_proj,
    step_size,
    decay_rate,
    bypass_factor,
    queries,
    turn_kv,
):
    parties = lax.axis_size("pool")
    segments = lax.axis_size("ctx")
    kv = kv_pool[0]
    pages = kv.shape[0]
    rows = queries.shape[1]
    heads = kv.shape[-1] // HEAD_DIM
    partner = [(i, i ^ 1) for i in range(segments)]
    opposite = [(i, i ^ 2) for i in range(segments)]

    def to_partner(array):
        return lax.ppermute(array, "ctx", partner)

    def to_opposite(array):
        return lax.ppermute(array, "ctx", opposite)

    if parties == 2:
        swap = [(0, 1), (1, 0)]
        moved, pieces, rest = [], [], kv
        for head in range(heads):
            columns = slice(head * HEAD_DIM, (head + 1) * HEAD_DIM)
            cut = rest[..., columns]
            if head:
                cut = jnp.concatenate([cut, cut[:1]], axis=0)
            cut = (cut,)
            cut, rest = lax.optimization_barrier((cut, rest))
            pieces.append(cut)
            moved.append(tuple(lax.ppermute(piece, "pool", swap) for piece in cut))
        table = block_owner * OWNER + block_index
    else:
        table = jnp.arange(pages, dtype=jnp.int32)[None]
        routed, slab = route_blocks(kv, state_pool, block_owner[0], block_index[0])
        moved = [(routed[..., h * HEAD_DIM : (h + 1) * HEAD_DIM],) for h in range(heads)]
    asks = (queries[0], to_opposite(queries[0]))

    turns = (turn_kv[0], to_partner(turn_kv[0]))
    tables = (table, to_partner(table))
    y, s, run = mixer_from_zero(
        turn_len, mixer_in[0], input_proj[0], output_proj[0], step_size[0], decay_rate, bypass_factor
    )
    parts = []
    after = run
    marks = (history_len, *tables)
    for head in range(heads):
        came, after = lax.optimization_barrier((moved[head], after))
        own_kv, partner_kv = (came,), (tuple(to_partner(piece) for piece in came),)
        if parties == 2:
            beside = tuple(to_partner(piece) for piece in pieces[head])
            own_kv, partner_kv = (pieces[head],) + own_kv, (beside,) + partner_kv
        ask = functools.partial(
            attend,
            head,
            pages=pages,
            marks=marks,
            queries=asks,
            own_kv=own_kv,
            partner_kv=partner_kv,
            turns=turns,
        )
        if head + 1 < heads:
            states = state_pool if parties == 2 and head == 0 else None
            sent, o, after, *padded, hidden, chosen = ask(sides=(1, 0), after=after, states=states)
            marks = (hidden, chosen)
            if padded:
                ordered = padded[0]
                slab = lax.ppermute(ordered, "pool", swap)
        else:
            (sent,) = ask(sides=(1,), after=after)
            o, after = ask(sides=(0,), after=sent)
        parts.append((o, after, to_opposite(sent)))
    slab, after = lax.optimization_barrier((slab, after))
    slabs = (ordered, slab) if parties == 2 else (slab,)
    mixed, final, after = add_saved(after, turn_len, chosen, slabs, y, s, run, output_proj[0])
    attended = None
    for head in range(heads):
        attended = merge(head, heads, after, turn_len, parts[head], rows, attended)
    return (mixed[None], final[None], attended[None])


def solution(mesh):
    return jax.shard_map(
        local,
        mesh=mesh,
        in_specs=(
            P("ctx", "pool", None, None, "head"),
            P("pool", "ctx", "head"),
            P("ctx", None),
            P("ctx", None),
            P("pool"),
            P("pool"),
            P("pool", "head", "ctx", None),
            P("pool", "head", None, None),
            P("pool", "head", None, None),
            P("pool", "head", None),
            P("head"),
            P("head"),
            P("pool", "ctx", "head"),
            P("pool", None, "ctx", "head"),
        ),
        out_specs=(
            P("pool", "head", "ctx", None),
            P("pool", "head", "ctx", None),
            P("pool", "ctx", "head"),
        ),
        check_vma=False,
    )
```
